32 devices in a mesh: term: 8 (over z, core), doc: 4 (over y, x).
Axes of the slice: x: 2, y: 2, z: 4, core: 2. Of those that a mesh axis runs over, the one named last changes fastest.
Arguments:
- tiles: float32 [4096, 128, 128], P(('term', 'doc')), may hold values from 0.01 to 1
- tile_coords: int32 [4096, 2], P(('term', 'doc')), may hold values from 0 to 63, as said below
- sketch_matrix: float32 [8192, 256], P('doc'), may hold values from -0.1875 to 0.1875
- anchor_terms: int32 [64], replicated, may hold values from 0 to 8191, as said below
Outputs:
- coefficients: float32 [8192, 64], P(('term', 'doc'))
- residual: float32 [8192, 256], P(('term', 'doc'))
The draws below stay inside these ranges and needn't reach their ends.
Inputs may be any that keep to these rules, and one draw needn't show every extreme that they name: `tile_coords`: column 0 is a term block below 64, column 1 a document block below 64. The tiles of the k-th device along term+doc (doc fastest) lie in document blocks j * 16 to j * 16 + 15, j being that device's doc index, and that device holds a tile of each of them. The term blocks fall in groups of 2 consecutive ones, the rows of one device along term+doc; the tiles of one device touch at most one term block of each group. Every term block holds a tile. Coordinates may repeat; such tiles add. `anchor_terms`: 64 distinct term rows; the last term row is always among them.
All inputs are finite; a program needn't handle non-finite values.
Results may differ from the reference program's by a relative error of at most 0.0003.
Values sent between devices are 32-bit elements; how exact they have to be, the bound alone decides.
No kernel may reach another device: no remote copies, remote signals or barrier semaphores. Data moves between devices by JAX's collectives and lax.ppermute only.
A program may use at most 256 MiB of HBM per device.

```python
import math
import jax
import jax.numpy as jnp
from jax import lax

TILE = 128
SKETCH = 256
ANCHORS = 64
TILES_DEV = 128
DB_DEV = 16
ROWS_DEV = 256
TERMS = 8192
DOCS = 8192
NTILES = 4096
N_TERM = 8
N_DOC = 4


def draw_tile_coords(key, part):
    devices = N_TERM * N_DOC
    total = TILES_DEV * devices
    per_owner = ROWS_DEV // TILE
    key_one, key_two, key_three, key_four = jax.random.split(key, 4)
    index = jnp.arange(total, dtype=jnp.int32)
    device = index // TILES_DEV
    local = index % TILES_DEV
    first = jax.random.randint(key_one, (total,), 0, devices)
    second = jax.random.randint(key_two, (total,), 0, devices)
    forced = device // per_owner + local * (devices // per_owner)
    owner = jnp.where(local < per_owner, forced, jnp.minimum(first, second)).astype(jnp.int32)
    shifts = jax.random.randint(key_three, (devices,), 0, per_owner)
    pick = (jnp.take(shifts, owner) + device) % per_owner
    term_block = owner * per_owner + pick
    doc_index = device % N_DOC
    spare = jax.random.randint(key_four, (total,), 0, DB_DEV)
    doc_block = doc_index * DB_DEV + jnp.where(local < DB_DEV, local, spare)
    return jnp.stack([term_block, doc_block], axis=1).astype(jnp.int32)


def draw_anchor_terms(key, part):
    order = jax.random.permutation(key, TERMS - 1)[:ANCHORS - 1].astype(jnp.int32)
    return jnp.concatenate([order, jnp.full((1,), TERMS - 1, jnp.int32)])


def levels(own_key, dims, cuts, smallest, high):
    level = 1.0
    for axis_at, shards_of in cuts:
        heights = jax.random.uniform(jax.random.fold_in(jax.random.fold_in(own_key, 6), axis_at), (shards_of,), jnp.float32, smallest / len(cuts), high / len(cuts))
        level = level * jnp.repeat(jnp.exp(heights), dims[axis_at] // shards_of).reshape((-1,) + (1,) * (len(dims) - 1 - axis_at))
    return level


def normal_values(stream_key, dims, scale, limit, cuts=(), kind=jnp.bfloat16):
    entries = jax.random.normal(stream_key, dims, jnp.float32) * scale
    if len(cuts) > 0:
        entries = levels(stream_key, dims, cuts, -0.22, 0.18) * entries
    return jnp.clip(entries, min=-limit, max=limit).astype(kind)


def setup_inputs(seed: int = 0) -> dict:
    key_list = jax.random.split(jax.random.key(seed), 5)
    tiles = jnp.clip(jnp.exp(math.log(1.0) - 4.6051702 * jax.random.uniform(key_list[0], (NTILES, TILE, TILE), jnp.float32) ** levels(key_list[0], (NTILES, TILE, TILE), ((0, 32),), -0.2, 0.2)), 0.01, 1.0)
    tile_coords = draw_tile_coords(jax.random.fold_in(key_list[4], 71), 0)
    sketch_matrix = normal_values(key_list[2], (DOCS, SKETCH), (8 * TILE) ** -0.5, 0.1875, ((0, 4),), jnp.float32)
    anchor_terms = draw_anchor_terms(jax.random.fold_in(key_list[4], 71), 0)
    return dict(tiles=tiles, tile_coords=tile_coords, sketch_matrix=sketch_matrix, anchor_terms=anchor_terms)


def reference(tiles, tile_coords, sketch_matrix, anchor_terms):
    blocks = TERMS // TILE
    width = sketch_matrix.shape[1]
    g_blocks = sketch_matrix.reshape(-1, TILE, width)
    steps = tiles.shape[0] // TILES_DEV
    tile_groups = tiles.reshape(steps, TILES_DEV, TILE, TILE)
    coord_groups = tile_coords.reshape(steps, TILES_DEV, 2)

    def step(total, inputs):
        pieces, coords = inputs
        chosen = jnp.take(g_blocks, coords[:, 1], axis=0)
        prods = jnp.einsum('kab,kbc->kac', pieces, chosen, precision=lax.Precision.HIGHEST)
        return (total + jax.ops.segment_sum(prods, coords[:, 0], num_segments=blocks), None)
    start = jnp.zeros((blocks, TILE, width), sketch_matrix.dtype)
    summed, unused = lax.scan(step, start, (tile_groups, coord_groups))
    sketch = summed.reshape(TERMS, width)
    anchor_rows = jnp.take(sketch, anchor_terms, axis=0)
    gram = jnp.dot(anchor_rows, anchor_rows.T, precision=lax.Precision.HIGHEST)
    ridge = 0.001 * jnp.trace(gram) / ANCHORS
    gram = gram + ridge * jnp.eye(ANCHORS, dtype=gram.dtype)
    factor = jnp.linalg.cholesky(gram)
    project = jnp.dot(sketch, anchor_rows.T, precision=lax.Precision.HIGHEST)
    coefficients = jax.scipy.linalg.cho_solve((factor, True), project.T).T
    residual = sketch - jnp.dot(coefficients, anchor_rows, precision=lax.Precision.HIGHEST)
    return (coefficients, residual)
```

```python
import functools

import jax
import jax.numpy as jnp
from jax import lax
from jax.experimental import pallas as pl
from jax.experimental.pallas import tpu as pltpu
from jax.sharding import PartitionSpec as P

ROWS_DEV = 256
NBUF = 8
F32 = jnp.float32
BF16 = jnp.bfloat16
AXES = ("term", "doc")


def split(v):
    hi = v.astype(BF16)
    lo = (v - hi.astype(F32)).astype(BF16)
    return hi, lo


def round8(n):
    return (n + 7) // 8 * 8


def chunk_kernel(geo, coords, anchors, me_ref, g_ref, tiles, *rest):
    (z_lo, nz, n_y, n_tiles, tile, half) = geo
    n_y_out = n_y - 1
    keep_x, send_x, keep_y = rest[:3]
    send_y = rest[3 : 3 + n_y_out]
    anchor_out = rest[3 + n_y_out]
    buf, order, acc_x, acc_y, flag_x, flag_y, in_sem, out_sem = rest[4 + n_y_out :]
    n_doc = 2 * n_y
    per = ROWS_DEV // tile
    sx = 2 * n_y * nz
    sy = 4 * nz
    fx = round8(sx)
    fy = round8(sy)
    me = me_ref[0]
    doc_base = me_ref[1]

    def place(block):
        rel = lax.bitwise_xor(block // per, me)
        dx = rel & 1
        dy = (rel >> 1) & (n_y - 1)
        dc = (rel // n_doc) & 1
        zi = (rel // (2 * n_doc)) - z_lo
        inside = jnp.logical_and(zi >= 0, zi < nz)
        in_x = (dc * n_y + dy) * nz + zi
        in_y = (dc * 2 + dx) * nz + zi
        return inside, dx, in_x, dy, in_y

    def fetch(index, slot):
        return pltpu.make_async_copy(tiles.at[index], buf.at[slot], in_sem.at[slot])

    def scan(k, count):
        inside = place(coords[k, 0])[0]

        @pl.when(inside)
        def _():
            order[count] = k

            @pl.when(count < NBUF)
            def _():
                fetch(k, count).start()

        return count + inside.astype(jnp.int32)

    count = lax.fori_loop(0, n_tiles, scan, jnp.int32(0))
    acc_x[...] = jnp.zeros_like(acc_x)
    acc_y[...] = jnp.zeros_like(acc_y)
    flag_x[...] = jnp.zeros_like(flag_x)
    flag_y[...] = jnp.zeros_like(flag_y)
    width = g_ref.shape[1]

    def step(i, carry):
        k = order[i]
        slot = lax.rem(i, NBUF)
        block = coords[k, 0]
        doc = coords[k, 1] - doc_base
        _, dx, in_x, dy, in_y = place(block)
        fetch(k, slot).wait()
        hi, lo = split(buf[slot])
        g_hi, g_lo = split(g_ref[pl.ds(pl.multiple_of(doc * tile, tile), tile), :])
        lhs = jnp.concatenate([hi, lo], axis=1)
        top = jnp.dot(lhs, jnp.concatenate([g_hi, g_hi], axis=0), preferred_element_type=F32)
        low = jnp.dot(lhs, jnp.concatenate([g_lo, g_lo], axis=0), preferred_element_type=F32)
        prod = top + low
        px = dx * sx + in_x
        py = dy * sy + in_y
        acc_x[px] += prod[:half]
        acc_y[py] += prod[half:]
        bit = jnp.full((1, width), lax.rem(block, per).astype(F32), F32)
        flag_x[pl.ds(dx * fx + in_x, 1), :] = bit
        flag_y[pl.ds(dy * fy + in_y, 1), :] = bit

        @pl.when(i + NBUF < count)
        def _():
            fetch(order[i + NBUF], slot).start()

        return carry

    lax.fori_loop(0, count, step, 0)
    copies = []

    def out(src, dst):
        copies.append(pltpu.make_async_copy(src, dst, out_sem.at[len(copies)]))
        copies[-1].start()

    for d, ref in enumerate((keep_x, send_x)):
        out(acc_x.at[pl.ds(d * sx, sx)], ref.at[pl.ds(0, sx)])
        out(flag_x.at[pl.ds(d * fx, fx)], ref.at[sx, pl.ds(0, fx)])
    for d, ref in enumerate((keep_y,) + tuple(send_y)):
        out(acc_y.at[pl.ds(d * sy, sy)], ref.at[pl.ds(0, sy)])
        out(flag_y.at[pl.ds(d * fy, fy)], ref.at[sy, pl.ds(0, fy)])

    def pick(i, carry):
        row = anchors[i]
        block = row // tile
        inside, dx, in_x, dy, in_y = place(block)
        line = lax.rem(row, tile)
        bit = lax.rem(block, per).astype(F32)

        @pl.when(jnp.logical_and(inside, line < half))
        def _():
            value = acc_x[dx * sx + in_x, pl.ds(line, 1), :]
            mine = flag_x[pl.ds(dx * fx + in_x, 1), :] == bit
            anchor_out[pl.ds(i, 1), :] = jnp.where(mine, value, 0.0)

        @pl.when(jnp.logical_and(inside, line >= half))
        def _():
            value = acc_y[dy * sy + in_y, pl.ds(line - half, 1), :]
            mine = flag_y[pl.ds(dy * fy + in_y, 1), :] == bit
            anchor_out[pl.ds(i, 1), :] = jnp.where(mine, value, 0.0)

        return carry

    anchor_out[...] = jnp.zeros_like(anchor_out)
    lax.fori_loop(0, anchors.shape[0], pick, 0)
    for copy in copies:
        copy.wait()


def chunk_products(z_lo, nz, n_y, coords, anchors, me, g, tiles):
    n_tiles, tile = tiles.shape[0], tiles.shape[1]
    width = g.shape[1]
    half = tile // 2
    sx, sy = 2 * n_y * nz, 4 * nz
    fx, fy = round8(sx), round8(sy)
    shape_x = jax.ShapeDtypeStruct((sx + 1, half, width), F32)
    shape_y = jax.ShapeDtypeStruct((sy + 1, half, width), F32)
    outs = [shape_x, shape_x] + [shape_y] * n_y + [jax.ShapeDtypeStruct((anchors.shape[0], width), F32)]
    anyspace = pl.BlockSpec(memory_space=pl.ANY)
    smem = pl.BlockSpec(memory_space=pltpu.SMEM)
    vmem = pl.BlockSpec(memory_space=pltpu.VMEM)
    return pl.pallas_call(
        functools.partial(chunk_kernel, (z_lo, nz, n_y, n_tiles, tile, half)),
        out_shape=outs,
        in_specs=[smem, smem, smem, vmem, anyspace],
        out_specs=[anyspace] * (2 + n_y) + [vmem],
        scratch_shapes=[
            pltpu.VMEM((NBUF, tile, tile), F32),
            pltpu.SMEM((n_tiles,), jnp.int32),
            pltpu.VMEM((2 * sx, half, width), F32),
            pltpu.VMEM((n_y * sy, half, width), F32),
            pltpu.VMEM((2 * fx, width), F32),
            pltpu.VMEM((n_y * fy, width), F32),
            pltpu.SemaphoreType.DMA((NBUF,)),
            pltpu.SemaphoreType.DMA((2 * (2 + n_y),)),
        ],
        compiler_params=pltpu.CompilerParams(vmem_limit_bytes=48 * 2**20),
        cost_estimate=pl.CostEstimate(flops=n_tiles * 2 * tile * tile * width, bytes_accessed=8 * 2**20, transcendentals=0),
    )(coords, anchors, me, g, tiles)


def spread_kernel(sx, sy, n_in, *refs):
    xs = refs[:2]
    ys = refs[2:n_in]
    keep, send = refs[n_in:]
    for parts, slots, base in ((xs, sx, 0), (ys, sy, sx // 2)):
        for j in range(slots):
            one = None
            zero = None
            for ref in parts:
                value = ref[j]
                flag = ref[slots, pl.ds(j, 1), :]
                up = value * flag
                down = value - up
                one = up if one is None else one + up
                zero = down if zero is None else zero + down
            core, rest = divmod(j, slots // 2)
            dst = send if core else keep
            dst[2 * (base + rest)] = zero
            dst[2 * (base + rest) + 1] = one


def spread(sx, sy, keep_x, recv_x, keep_y, recv_y):
    half, width = keep_x.shape[1:]
    shape = jax.ShapeDtypeStruct((sx + sy, half, width), F32)
    args = (keep_x, recv_x, keep_y) + tuple(recv_y)
    vmem = pl.BlockSpec(memory_space=pltpu.VMEM)
    return pl.pallas_call(
        functools.partial(spread_kernel, sx, sy, len(args)),
        out_shape=[shape, shape],
        in_specs=[vmem] * len(args),
        out_specs=[vmem, vmem],
        compiler_params=pltpu.CompilerParams(vmem_limit_bytes=48 * 2**20),
    )(*args)


def hdot(a, b, dims):
    return lax.dot_general(a, b, (dims, ((), ())), precision=lax.Precision.HIGHEST, preferred_element_type=F32)


def finish_kernel(n_whole, half, *refs):
    parts = refs[:n_whole]
    rows_ref, inv_ref, coef_ref, res_ref = refs[n_whole:]
    total = parts[0][...]
    for ref in parts[1:]:
        total = total + ref[...]
    owned = jnp.concatenate([total[0, 0], total[1, 0], total[0, 1], total[1, 1]], axis=0)
    rows = rows_ref[...]
    project = hdot(owned, rows, ((1,), (1,)))
    coef = hdot(project, inv_ref[...], ((1,), (0,)))
    coef_ref[...] = coef
    res_ref[...] = owned - hdot(coef, rows, ((1,), (0,)))


def finish(parts, rows, inv):
    half, width = parts[0].shape[2:]
    vmem = pl.BlockSpec(memory_space=pltpu.VMEM)
    return pl.pallas_call(
        functools.partial(finish_kernel, len(parts), half),
        out_shape=[jax.ShapeDtypeStruct((4 * half, rows.shape[0]), F32), jax.ShapeDtypeStruct((4 * half, width), F32)],
        in_specs=[vmem] * (len(parts) + 2),
        out_specs=[vmem, vmem],
        compiler_params=pltpu.CompilerParams(vmem_limit_bytes=32 * 2**20),
    )(*parts, rows, inv)


def make_chunks(n_z):
    step = max(1, n_z // 2)
    return [(lo, step) for lo in range(n_z - step, -1, -step)]


def body(n_term, n_doc, tiles, coords, sketch, anchors):
    devices = n_term * n_doc
    n_y, n_z = n_doc // 2, n_term // 2
    me = lax.axis_index(AXES).astype(jnp.int32)
    doc_base = lax.axis_index("doc").astype(jnp.int32) * (sketch.shape[0] // tiles.shape[1])
    me_arr = jnp.stack([me, doc_base])

    def swap(v, mask):
        return lax.ppermute(v, AXES, [(i, i ^ mask) for i in range(devices)])

    half, width = tiles.shape[1] // 2, sketch.shape[1]
    whole = [None] * n_z
    anchor_parts = []
    for z_lo, nz in make_chunks(n_z):
        sx, sy = 2 * n_y * nz, 4 * nz
        keep_x, send_x, keep_y, *rest = chunk_products(z_lo, nz, n_y, coords, anchors, me_arr, sketch, tiles)
        send_y, part = rest[:-1], rest[-1]
        anchor_parts.append(part)
        recv_x = swap(send_x, 1)
        recv_y = [swap(v, 2 * (k + 1)) for k, v in enumerate(send_y)]
        keep, send = spread(sx, sy, keep_x, recv_x, keep_y, recv_y)
        got = swap(send, n_doc)
        n = 2 * nz
        pieces = [keep[i * n : (i + 1) * n] + got[i * n : (i + 1) * n] for i in range(n_y + 2)]
        xs, ys = pieces[:n_y], pieces[n_y:]
        total_x = xs[0]
        for k in range(1, n_y):
            total_x = total_x + swap(xs[k], 2 * k)
        total_y = ys[0] + swap(ys[1], 1)
        both = jnp.stack([total_x.reshape(nz, 2, half, width), total_y.reshape(nz, 2, half, width)], axis=1)
        for zi in range(nz):
            dz = z_lo + zi
            whole[dz] = swap(both[zi], dz * 2 * n_doc) if dz else both[zi]
    rows = sum(anchor_parts[1:], anchor_parts[0])
    mask = n_doc
    while mask < devices:
        rows = rows + swap(rows, mask)
        mask *= 2
    mask = 1
    while mask < n_doc:
        rows = rows + swap(rows, mask)
        mask *= 2
    count = rows.shape[0]
    gram = jnp.dot(rows, rows.T, precision=lax.Precision.HIGHEST)
    ridge = 0.001 * jnp.trace(gram) / count
    eye = jnp.eye(count, dtype=F32)
    factor = jnp.linalg.cholesky(gram + ridge * eye)
    inv = jax.scipy.linalg.cho_solve((factor, True), eye)
    coef, res = finish(whole, rows, inv)
    return (coef, res)


def solution(mesh):
    in_specs = (P(("term", "doc"), None, None), P(("term", "doc"), None), P("doc", None), P())
    out_specs = (P(("term", "doc"), None), P(("term", "doc"), None))
    run = functools.partial(body, mesh.shape["term"], mesh.shape["doc"])
    return jax.shard_map(run, mesh=mesh, in_specs=in_specs, out_specs=out_specs, check_vma=False)
```

```python
import functools

import jax
import jax.numpy as jnp
from jax import lax
from jax.experimental import pallas as pl
from jax.experimental.pallas import tpu as pltpu
from jax.sharding import PartitionSpec as P

ROWS_DEV = 256
UNROLL = 8
F32 = jnp.float32
BF16 = jnp.bfloat16
AXES = ("term", "doc")
TOKEN = (8, 128)
LIMIT = pltpu.CompilerParams(vmem_limit_bytes=48 * 2**20)
TINY = pl.CostEstimate(flops=1, bytes_accessed=1, transcendentals=0)
ANY = pl.BlockSpec(memory_space=pl.ANY)
HBM = pl.BlockSpec(memory_space=pltpu.HBM)
SMEM = pl.BlockSpec(memory_space=pltpu.SMEM)
VMEM = pl.BlockSpec(memory_space=pltpu.VMEM)


def shaped(shape, dtype=F32):
    return jax.ShapeDtypeStruct(tuple(shape), dtype)


def split(v):
    hi = v.astype(BF16)
    lo = (v - hi.astype(F32)).astype(BF16)
    return hi, lo


def hdot(a, b, dims):
    return lax.dot_general(a, b, (dims, ((), ())), precision=lax.Precision.HIGHEST, preferred_element_type=F32)


def in_order(kernel, last, _token, *refs):
    kernel(*refs[:last], *refs[last + 1 :])
    refs[last][...] = jnp.zeros_like(refs[last])


class Queue:
    def __init__(self, token):
        self.token = token

    def call(self, name, kernel, out_shape, args):
        got = pl.pallas_call(
            functools.partial(in_order, kernel, len(args)),
            out_shape=(shaped(TOKEN),) + tuple(out_shape),
            in_specs=[VMEM] * (1 + len(args)),
            out_specs=(VMEM,) * (1 + len(out_shape)),
            compiler_params=LIMIT,
            cost_estimate=TINY,
            name=name,
        )(self.token, *args)
        self.token = got[0]
        return got[1:]


def products_kernel(geo, first, coords, anchors, me_ref, tiles, *rest):
    n_y, n_z, n_tiles, tile = geo
    if first:
        g_hbm, blocks, anchor_out, wide, buf, order, flag, in_sem, g_ref, g_sem = rest
        load = pltpu.make_async_copy(g_hbm, g_ref, g_sem)
        load.start()
    else:
        wide, anchor_in, blocks, anchor_out, token, buf, order, flag, in_sem = rest
        token[...] = jnp.zeros_like(token)
    n_doc = 2 * n_y
    slots = n_z * n_doc
    per = ROWS_DEV // tile
    me = me_ref[0]
    doc_base = me_ref[1]
    width = wide.shape[1] // 2

    def place(block):
        rel = lax.bitwise_xor(block // per, me)
        dc = (rel // n_doc) & 1
        mine = dc == (1 if first else 0)
        slot = (rel // (2 * n_doc)) * n_doc + lax.rem(rel, n_doc)
        return mine, slot

    def scan(k, count):
        order[count] = k
        return count + place(coords[0, k])[0].astype(jnp.int32)

    count = lax.fori_loop(0, n_tiles, scan, jnp.int32(0), unroll=8)
    groups = (count + UNROLL - 1) // UNROLL

    def entry(i):
        valid = i < count
        return valid, jnp.where(valid, order[jnp.minimum(i, n_tiles - 1)], 0)

    def fetch(j, u):
        at = lax.rem(j, 2) * UNROLL + u
        return pltpu.make_async_copy(tiles.at[entry(j * UNROLL + u)[1]], buf.at[at], in_sem.at[at])

    def fetch_group(j):
        @pl.when(j < groups)
        def _():
            for u in range(UNROLL):
                fetch(j, u).start()

    fetch_group(0)
    blocks[...] = jnp.zeros_like(blocks)
    flag[...] = jnp.zeros_like(flag)
    if first:
        load.wait()
        hi, lo = split(g_ref[...])
        wide[:, :width] = hi
        wide[:, width:] = lo

    def product(j, u):
        valid, k = entry(j * UNROLL + u)
        doc = coords[1, k] - doc_base
        hi, lo = split(buf[lax.rem(j, 2) * UNROLL + u])
        w = wide[pl.ds(pl.multiple_of(doc * tile, tile), tile), :]
        lhs = jnp.concatenate([hi, lo], axis=1)
        both = jnp.dot(lhs, jnp.concatenate([w, w], axis=0), preferred_element_type=F32)
        return both[:, :width] + both[:, width:]

    def group(j, carry):
        fetch_group(j + 1)
        for u in range(UNROLL):
            fetch(j, u).wait()
        prods = [product(j, u) for u in range(UNROLL)]
        for u, prod in enumerate(prods):
            valid, k = entry(j * UNROLL + u)
            block = coords[0, k]
            slot = jnp.where(valid, place(block)[1], slots)
            blocks[slot] += prod
            flag[pl.ds(slot, 1), :] = jnp.full((1, width), lax.rem(block, per).astype(F32), F32)
        return carry

    lax.fori_loop(0, groups, group, 0)
    if first:
        anchor_out[...] = jnp.zeros_like(anchor_out)
    else:
        anchor_out[...] = anchor_in[...]

    def pick(i, carry):
        row = anchors[i]
        block = row // tile
        mine, slot = place(block)

        @pl.when(mine)
        def _():
            value = blocks[slot, pl.ds(lax.rem(row, tile), 1), :]
            same = flag[pl.ds(slot, 1), :] == lax.rem(block, per).astype(F32)
            anchor_out[pl.ds(i, 1), :] = jnp.where(same, value, 0.0)

        return carry

    lax.fori_loop(0, anchors.shape[0], pick, 0)
    blocks[slots, pl.ds(0, slots), :] = flag[pl.ds(0, slots), :]


def products(n_y, n_z, coords, anchors, me, tiles, g=None, wide=None, anchor_in=None):
    n_tiles, tile = tiles.shape[:2]
    first = g is not None
    width = g.shape[1] if first else wide.shape[1] // 2
    slots = n_z * 2 * n_y
    outs = [shaped((slots + 1, tile, width)), shaped((anchors.shape[0], width))]
    scratch = [
        pltpu.VMEM((2 * UNROLL, tile, tile), F32),
        pltpu.SMEM((n_tiles + 8,), jnp.int32),
        pltpu.VMEM((slots + 8, width), F32),
        pltpu.SemaphoreType.DMA((2 * UNROLL,)),
    ]
    if first:
        outs.append(shaped((g.shape[0], 2 * width), BF16))
        scratch += [pltpu.VMEM(g.shape, F32), pltpu.SemaphoreType.DMA]
        more, specs = (g,), [HBM]
    else:
        outs.append(shaped(TOKEN))
        more, specs = (wide, anchor_in), [VMEM, VMEM]
    return pl.pallas_call(
        functools.partial(products_kernel, (n_y, n_z, n_tiles, tile), first),
        out_shape=outs,
        in_specs=[SMEM, SMEM, SMEM, HBM] + specs,
        out_specs=[VMEM] * 3,
        scratch_shapes=scratch,
        compiler_params=LIMIT,
        cost_estimate=pl.CostEstimate(flops=8 * 10**9, bytes_accessed=5 * 2**20, transcendentals=0),
        name="products_away" if first else "products_here",
    )(coords, anchors, me, tiles, *more)


def spread_kernel(dz, n_y, own, got, stay, send_x, *send_y):
    slots = own.shape[0] - 1
    half = own.shape[1] // 2
    for dy in range(n_y):
        for dx in range(2):
            slot = (dz * n_y + dy) * 2 + dx
            a, b = own[slot], got[slot]
            up_a = a * own[slots, pl.ds(slot, 1), :]
            up_b = b * got[slots, pl.ds(slot, 1), :]
            for s, value in enumerate(((a - up_a) + (b - up_b), up_a + up_b)):
                if dx:
                    send_x[2 * dy + s] = value[:half]
                else:
                    stay[2 * dy + s] = value[:half]
                if dy:
                    send_y[dy - 1][2 * dx + s] = value[half:]
                else:
                    stay[2 * n_y + 2 * dx + s] = value[half:]


def spread(queue, dz, n_y, own, got):
    half, width = own.shape[1] // 2, own.shape[2]
    outs = (shaped((2 * n_y + 4, half, width)), shaped((2 * n_y, half, width))) + (shaped((4, half, width)),) * (n_y - 1)
    stay, send_x, *send_y = queue.call("spread", functools.partial(spread_kernel, dz, n_y), outs, (own, got))
    return stay, send_x, send_y


def join_kernel(n_y, stay, got_x, *refs):
    got_y = refs[: n_y - 1]
    keep, send_x = refs[n_y - 1 : n_y + 1]
    send_y = refs[n_y + 1 :]
    for dy in range(n_y):
        for s in range(2):
            value = stay[2 * dy + s] + got_x[2 * dy + s]
            if dy:
                send_y[dy - 1][s] = value
            else:
                keep[s] = value
    for dx in range(2):
        for s in range(2):
            value = stay[2 * n_y + 2 * dx + s]
            for ref in got_y:
                value = value + ref[2 * dx + s]
            if dx:
                send_x[s] = value
            else:
                keep[2 + s] = value


def join(queue, n_y, stay, got_x, got_y):
    half, width = stay.shape[1:]
    outs = (shaped((4, half, width)),) + (shaped((2, half, width)),) * n_y
    keep, send_x, *send_y = queue.call("join", functools.partial(join_kernel, n_y), outs, (stay, got_x, *got_y))
    return keep, send_x, send_y


def merge_kernel(n_y, keep, got_x, *refs):
    got_y, far, out = refs[: n_y - 1], refs[n_y - 1 : -1], refs[-1]
    x, y = keep[:2], keep[2:] + got_x[...]
    for ref in got_y:
        x = x + ref[...]
    for ref in far:
        x = x + ref[:2]
        y = y + ref[2:]
    out[:2] = x
    out[2:] = y


def merge(queue, n_y, keep, got_x, got_y, far=()):
    return queue.call("merge", functools.partial(merge_kernel, n_y), (shaped(keep.shape),), (keep, got_x, *got_y, *far))[0]


def total_kernel(*refs):
    total = refs[0][...]
    for ref in refs[1:-1]:
        total = total + ref[...]
    refs[-1][...] = total


def total(queue, values):
    return queue.call("total", total_kernel, (shaped(values[0].shape),), values)[0]


def inverse_kernel(n_in, *refs):
    ins, (rows_ref, inv_ref) = refs[:n_in], refs[n_in:]
    rows = ins[0][...]
    for ref in ins[1:]:
        rows = rows + ref[...]
    rows_ref[...] = rows
    count = rows.shape[0]
    m = hdot(rows, rows, ((1,), (1,)))
    at_row = lax.broadcasted_iota(jnp.int32, (count, count), 0)
    at_col = lax.broadcasted_iota(jnp.int32, (count, count), 1)
    diagonal = at_row == at_col
    ridge = 0.001 * jnp.sum(jnp.where(diagonal, m, 0.0)) / count
    m = jnp.where(diagonal, m + ridge, m)
    for k in range(count):
        row = m[k : k + 1, :]
        col = m[:, k : k + 1]
        scale = 1.0 / m[k : k + 1, k : k + 1]
        row = jnp.where(at_col[:1] == k, 1.0, row) * scale
        m = jnp.where(at_row == k, row, jnp.where(at_col == k, 0.0, m) - col * row)
    inv_ref[...] = m


def inverse(queue, parts):
    count, width = parts[0].shape
    return queue.call("inverse", functools.partial(inverse_kernel, len(parts)), (shaped((count, width)), shaped((count, count))), parts)


def finish_kernel(n_far, near, *refs):
    x, y = near[:2], near[2:]
    for ref in refs[:n_far]:
        x = x + ref[:2]
        y = y + ref[2:]
    rows_ref, inv_ref, coef_ref, res_ref = refs[n_far:]
    owned = jnp.concatenate([x[0], y[0], x[1], y[1]], axis=0)
    rows = rows_ref[...]
    project = hdot(rows, owned, ((1,), (1,)))
    coef = hdot(inv_ref[...], project, ((1,), (0,)))
    coef_ref[...] = coef
    res_ref[...] = owned - hdot(coef, rows, ((0,), (0,)))


def finish(queue, near, far, rows, inv):
    half, width = near.shape[1:]
    outs = (shaped((rows.shape[0], 4 * half)), shaped((4 * half, width)))
    coef, res = queue.call("finish", functools.partial(finish_kernel, len(far)), outs, (near, *far, rows, inv))
    return coef.T, res


def body(n_term, n_doc, tiles, coords, sketch, anchors):
    devices = n_term * n_doc
    n_y, n_z = n_doc // 2, n_term // 2
    me = lax.axis_index(AXES).astype(jnp.int32)
    doc_base = lax.axis_index("doc").astype(jnp.int32) * (sketch.shape[0] // tiles.shape[1])
    where = jnp.stack([me, doc_base])

    def swap(v, mask):
        return lax.ppermute(v, AXES, [(i, i ^ mask) for i in range(devices)])

    def swap_y(values):
        return [swap(v, 2 * (k + 1)) for k, v in enumerate(values)]

    z_masks = [2 * n_doc * k for k in range(1, n_z)]
    away, part, wide = products(n_y, n_z, coords.T, anchors, where, tiles, g=sketch)
    got = swap(away, n_doc)
    here, part, token = products(n_y, n_z, coords.T, anchors, where, tiles, wide=wide, anchor_in=part)
    queue = Queue(token)
    first, second, far = {}, {}, {}

    def do_spread(dz):
        stay, send_x, send_y = spread(queue, dz, n_y, here, got)
        first[dz] = (stay, swap(send_x, 1), swap_y(send_y))

    def do_join(dz):
        keep, send_x, send_y = join(queue, n_y, *first.pop(dz))
        second[dz] = (keep, swap(send_x, 1), swap_y(send_y))

    def do_merge(dz, *more):
        far[dz] = swap(merge(queue, n_y, *second.pop(dz), more), 2 * n_doc * dz)

    top = n_z - 1
    do_spread(top)
    do_spread(top - 1)
    rounds = [part] + [swap(part, mask) for mask in z_masks]
    part = total(queue, rounds)
    rounds = [part] + [swap(part, mask) for mask in range(1, n_doc)]
    do_join(top)
    if top >= 2:
        do_spread(top - 2)
    do_join(top - 1)
    if top >= 3:
        do_spread(top - 3)
    for dz in range(top, 0, -1):
        do_merge(dz)
        if dz == top:
            part = total(queue, rounds)
            rounds = [part, swap(part, n_doc)]
        if dz >= 2:
            do_join(dz - 2)
        if dz >= 4:
            do_spread(dz - 4)
        if dz == 2:
            rows, inv = inverse(queue, rounds)
    if top < 2:
        rows, inv = inverse(queue, rounds)
    near = merge(queue, n_y, *second.pop(0), [far.pop(dz) for dz in range(top, 2, -1)])
    if 2 in far:
        near = total(queue, [near, far.pop(2)])
    return finish(queue, near, list(far.values()), rows, inv)


def solution(mesh):
    in_specs = (P(("term", "doc"), None, None), P(("term", "doc"), None), P("doc", None), P())
    out_specs = (P(("term", "doc"), None), P(("term", "doc"), None))
    run = functools.partial(body, mesh.shape["term"], mesh.shape["doc"])
    return jax.shard_map(run, mesh=mesh, in_specs=in_specs, out_specs=out_specs, check_vma=False)
```

```python
import functools

import jax
import jax.numpy as jnp
from jax import lax
from jax.experimental import pallas as pl
from jax.experimental.pallas import tpu as pltpu
from jax.sharding import PartitionSpec as P

ROWS_DEV = 256
UNROLL = 8
F32 = jnp.float32
BF16 = jnp.bfloat16
AXES = ("term", "doc")
TOKEN = (8, 128)
LIMIT = pltpu.CompilerParams(vmem_limit_bytes=24 * 2**20)
LARGE = pltpu.CompilerParams(vmem_limit_bytes=44 * 2**20)
TINY = pl.CostEstimate(flops=1, bytes_accessed=1, transcendentals=0)
ANY = pl.BlockSpec(memory_space=pl.ANY)
HBM = pl.BlockSpec(memory_space=pltpu.HBM)
SMEM = pl.BlockSpec(memory_space=pltpu.SMEM)
VMEM = pl.BlockSpec(memory_space=pltpu.VMEM)


def shaped(shape, dtype=F32):
    return jax.ShapeDtypeStruct(tuple(shape), dtype)


def split(v):
    hi = v.astype(BF16)
    lo = (v - hi.astype(F32)).astype(BF16)
    return hi, lo


def hdot(a, b, dims):
    return lax.dot_general(a, b, (dims, ((), ())), precision=lax.Precision.HIGHEST, preferred_element_type=F32)


def in_order(kernel, last, _token, *refs):
    kernel(*refs[:last], *refs[last + 1 :])
    refs[last][...] = jnp.zeros_like(refs[last])


class Queue:
    def __init__(self, token):
        self.token = token

    def call(self, name, kernel, out_shape, args):
        got = pl.pallas_call(
            functools.partial(in_order, kernel, len(args)),
            out_shape=(shaped(TOKEN),) + tuple(out_shape),
            in_specs=[VMEM] * (1 + len(args)),
            out_specs=(VMEM,) * (1 + len(out_shape)),
            compiler_params=LIMIT,
            cost_estimate=TINY,
            name=name,
        )(self.token, *args)
        self.token = got[0]
        return got[1:]


def products_kernel(slots, code_ref, tiles, top_ref, low_ref, *rest):
    if len(rest) == 7:
        away, (blocks, anchor_out, buf, order, flag, in_sem) = True, rest[1:]
        anchor_out[...] = jnp.zeros_like(anchor_out)
    else:
        away, (anchor_in, blocks, anchor_out, token, buf, order, flag, in_sem) = False, rest
        token[...] = jnp.zeros_like(token)
        anchor_out[...] = anchor_in[...]
    n_tiles, tile = tiles.shape[:2]
    width = top_ref.shape[1]

    def wanted(code):
        return ((code >> 10) & 1) == (1 if away else 0)

    def fetch(k, i):
        return pltpu.make_async_copy(tiles.at[k], buf.at[i], in_sem.at[i])

    def scan(k, count):
        code = code_ref[k]
        mine = wanted(code)
        order[count] = code

        @pl.when(mine)
        def _():
            fetch(k, count).start()

        return count + mine.astype(jnp.int32)

    count = lax.fori_loop(0, n_tiles, scan, jnp.int32(0), unroll=4)
    blocks[...] = jnp.zeros_like(blocks)
    flag[...] = jnp.zeros_like(flag)

    def product(i, code):
        hi, lo = split(buf[i])
        rows = pl.ds(pl.multiple_of((code >> 12) * tile, tile), tile)
        w = jnp.concatenate([top_ref[rows, :], low_ref[rows, :]], axis=1)
        lhs = jnp.concatenate([hi, lo], axis=1)
        both = jnp.dot(lhs, jnp.concatenate([w, w], axis=0), preferred_element_type=F32)
        return both[:, :width] + both[:, width:]

    def put(code, prod):
        slot = code & 1023
        blocks[slot] += prod
        flag[pl.ds(slot, 1), :] = jnp.full((1, width), ((code >> 11) & 1).astype(F32), F32)

    def several(base, many):
        for u in range(many):
            fetch(0, base + u).wait()
        codes = [order[base + u] for u in range(many)]
        prods = [product(base + u, codes[u]) for u in range(many)]
        for code, prod in zip(codes, prods):
            put(code, prod)

    whole = count // UNROLL

    def group(j, carry):
        several(j * UNROLL, UNROLL)
        return carry

    def single(i, carry):
        several(i, 1)
        return carry

    lax.fori_loop(0, whole, group, 0)
    lax.fori_loop(whole * UNROLL, count, single, 0)

    def pick(i, carry):
        code = code_ref[n_tiles + i]

        @pl.when(wanted(code))
        def _():
            slot = code & 1023
            value = blocks[slot, pl.ds(code >> 12, 1), :]
            same = flag[pl.ds(slot, 1), :] == ((code >> 11) & 1).astype(F32)
            anchor_out[pl.ds(i, 1), :] = jnp.where(same, value, 0.0)

        return carry

    lax.fori_loop(0, anchor_out.shape[0], pick, 0)
    blocks[slots, pl.ds(0, slots), :] = flag[pl.ds(0, slots), :]


def products(slots, codes, tiles, top, low, more):
    n_tiles, tile = tiles.shape[:2]
    width = top.shape[1]
    away = len(more) == 0
    outs = [shaped((slots + 1, tile, width)), shaped((codes.shape[0] - n_tiles, width))]
    if not away:
        outs.append(shaped(TOKEN))
    return pl.pallas_call(
        functools.partial(products_kernel, slots),
        out_shape=outs,
        in_specs=[SMEM, HBM, VMEM, VMEM] + [VMEM] * max(1, len(more)),
        out_specs=[VMEM] * len(outs),
        scratch_shapes=[
            pltpu.VMEM((n_tiles, tile, tile), F32),
            pltpu.SMEM((n_tiles + 8,), jnp.int32),
            pltpu.VMEM((slots + 8, width), F32),
            pltpu.SemaphoreType.DMA((n_tiles,)),
        ],
        compiler_params=LARGE,
        cost_estimate=pl.CostEstimate(flops=8 * 10**9, bytes_accessed=5 * 2**20, transcendentals=0),
        name="products_away" if away else "products_here",
    )(codes, tiles, top, low, *(more or (jnp.zeros(TOKEN, F32),)))


def encode(n_doc, me, block, extra, per):
    rel = lax.bitwise_xor(block // per, me)
    core = (rel // n_doc) & 1
    slot = (rel // (2 * n_doc)) * n_doc + (rel & (n_doc - 1))
    return slot | (core << 10) | ((block % per) << 11) | (extra << 12)


def spread_kernel(zs, n_y, own, got, stay, send_x, *send_y):
    slots = own.shape[0] - 1
    half = own.shape[1] // 2
    n_x = len(zs) * 2 * n_y
    for i, dz in enumerate(zs):
        for dy in range(n_y):
            for dx in range(2):
                slot = (dz * n_y + dy) * 2 + dx
                a, b = own[slot], got[slot]
                up_a = a * own[slots, pl.ds(slot, 1), :]
                up_b = b * got[slots, pl.ds(slot, 1), :]
                for s, value in enumerate(((a - up_a) + (b - up_b), up_a + up_b)):
                    at = 2 * (i * n_y + dy) + s
                    if dx:
                        send_x[at] = value[:half]
                    else:
                        stay[at] = value[:half]
                    at = 2 * (i * 2 + dx) + s
                    if dy:
                        send_y[dy - 1][at] = value[half:]
                    else:
                        stay[n_x + at] = value[half:]


def spread(queue, zs, n_y, own, got):
    half, width = own.shape[1] // 2, own.shape[2]
    n_x, n_yy = len(zs) * 2 * n_y, len(zs) * 4
    outs = (shaped((n_x + n_yy, half, width)), shaped((n_x, half, width))) + (shaped((n_yy, half, width)),) * (n_y - 1)
    stay, send_x, *send_y = queue.call("spread", functools.partial(spread_kernel, zs, n_y), outs, (own, got))
    return stay, send_x, send_y


def join_kernel(n, n_y, stay, got_x, *refs):
    got_y = refs[: n_y - 1]
    keep, send_x = refs[n_y - 1 : n_y + 1]
    send_y = refs[n_y + 1 :]
    n_x = n * 2 * n_y
    for i in range(n):
        for s in range(2):
            for dy in range(n_y):
                at = 2 * (i * n_y + dy) + s
                value = stay[at] + got_x[at]
                if dy:
                    send_y[dy - 1][2 * i + s] = value
                else:
                    keep[4 * i + s] = value
            for dx in range(2):
                at = 2 * (i * 2 + dx) + s
                value = stay[n_x + at]
                for ref in got_y:
                    value = value + ref[at]
                if dx:
                    send_x[2 * i + s] = value
                else:
                    keep[4 * i + 2 + s] = value


def join(queue, n, n_y, stay, got_x, got_y):
    half, width = stay.shape[1:]
    outs = (shaped((4 * n, half, width)),) + (shaped((2 * n, half, width)),) * n_y
    keep, send_x, *send_y = queue.call("join", functools.partial(join_kernel, n, n_y), outs, (stay, got_x, *got_y))
    return keep, send_x, send_y


def merge_kernel(n, n_y, n_far, keep, got_x, *refs):
    got_y, far, outs = refs[: n_y - 1], refs[n_y - 1 : n_y - 1 + n_far], refs[n_y - 1 + n_far :]
    for i, out in enumerate(outs):
        for s in range(2):
            x = keep[4 * i + s]
            y = keep[4 * i + 2 + s] + got_x[2 * i + s]
            for ref in got_y:
                x = x + ref[2 * i + s]
            if i == n - 1:
                for ref in far:
                    x = x + ref[s]
                    y = y + ref[2 + s]
            out[s] = x
            out[2 + s] = y


def merge(queue, n, n_y, keep, got_x, got_y, far=()):
    outs = (shaped((4,) + keep.shape[1:]),) * n
    return queue.call("merge", functools.partial(merge_kernel, n, n_y, len(far)), outs, (keep, got_x, *got_y, *far))


def total_kernel(*refs):
    total = refs[0][...]
    for ref in refs[1:-1]:
        total = total + ref[...]
    refs[-1][...] = total


def total(queue, values):
    return queue.call("total", total_kernel, (shaped(values[0].shape),), values)[0]


def inverse_kernel(n_in, *refs):
    ins, (rows_ref, inv_ref) = refs[:n_in], refs[n_in:]
    rows = ins[0][...]
    for ref in ins[1:]:
        rows = rows + ref[...]
    rows_ref[...] = rows
    count = rows.shape[0]
    m = hdot(rows, rows, ((1,), (1,)))
    at_row = lax.broadcasted_iota(jnp.int32, (count, count), 0)
    at_col = lax.broadcasted_iota(jnp.int32, (count, count), 1)
    diagonal = at_row == at_col
    ridge = 0.001 * jnp.sum(jnp.where(diagonal, m, 0.0)) / count
    m = jnp.where(diagonal, m + ridge, m)
    for k in range(count):
        row = m[k : k + 1, :]
        col = m[:, k : k + 1]
        scale = 1.0 / m[k : k + 1, k : k + 1]
        row = jnp.where(at_col[:1] == k, 1.0, row) * scale
        m = jnp.where(at_row == k, row, jnp.where(at_col == k, 0.0, m) - col * row)
    inv_ref[...] = m


def inverse(queue, parts):
    count, width = parts[0].shape
    return queue.call("inverse", functools.partial(inverse_kernel, len(parts)), (shaped((count, width)), shaped((count, count))), parts)


def finish_kernel(n_far, near, *refs):
    x, y = near[:2], near[2:]
    for ref in refs[:n_far]:
        x = x + ref[:2]
        y = y + ref[2:]
    rows_ref, inv_ref, coef_ref, res_ref = refs[n_far:]
    owned = jnp.concatenate([x[0], y[0], x[1], y[1]], axis=0)
    rows = rows_ref[...]
    project = hdot(rows, owned, ((1,), (1,)))
    coef = hdot(inv_ref[...], project, ((1,), (0,)))
    coef_ref[...] = coef
    res_ref[...] = owned - hdot(coef, rows, ((0,), (0,)))


def finish(queue, near, far, rows, inv):
    half, width = near.shape[1:]
    outs = (shaped((rows.shape[0], 4 * half)), shaped((4 * half, width)))
    coef, res = queue.call("finish", functools.partial(finish_kernel, len(far)), outs, (near, *far, rows, inv))
    return coef.T, res


def body(n_term, n_doc, tiles, coords, sketch, anchors):
    devices = n_term * n_doc
    n_y, n_z = n_doc // 2, n_term // 2
    tile, width = tiles.shape[1], sketch.shape[1]
    per = ROWS_DEV // tile
    me = lax.axis_index(AXES).astype(jnp.int32)
    doc_base = lax.axis_index("doc").astype(jnp.int32) * (sketch.shape[0] // tile)

    def swap(v, mask):
        return lax.ppermute(v, AXES, [(i, i ^ mask) for i in range(devices)])

    def swap_y(values):
        return [swap(v, 2 * (k + 1)) for k, v in enumerate(values)]

    codes = jnp.concatenate([
        encode(n_doc, me, coords[:, 0], coords[:, 1] - doc_base, per),
        encode(n_doc, me, anchors // tile, anchors % tile, per),
    ])
    top = lax.reduce_precision(sketch, 8, 7)
    low = (sketch - top).astype(BF16)
    top = top.astype(BF16)
    slots = n_z * n_doc
    away, part = products(slots, codes, tiles, top, low, ())
    got = swap(away, n_doc)
    here, part, token = products(slots, codes, tiles, top, low, (part,))
    queue = Queue(token)

    def do_spread(zs):
        stay, send_x, send_y = spread(queue, zs, n_y, here, got)
        return stay, swap(send_x, 1), swap_y(send_y)

    def do_join(zs, state):
        keep, send_x, send_y = join(queue, len(zs), n_y, *state)
        return keep, swap(send_x, 1), swap_y(send_y)

    far_zs, mid_zs = tuple(range(n_z - 1, n_z // 2 - 1, -1)), tuple(range(n_z // 2 - 1, 0, -1))
    far_state = do_spread(far_zs)
    masks = [n_doc << b for b in range((n_term - 1).bit_length())]
    for mask in masks:
        part = total(queue, [part, swap(part, mask)])
    rounds = [part, swap(part, 1)]
    far_state = do_join(far_zs, far_state)
    mid_state = do_spread(mid_zs)
    near_state = do_spread((0,))
    part = total(queue, rounds)
    for b in range(1, (n_doc - 1).bit_length() - 1):
        part = total(queue, [part, swap(part, 1 << b)])
    rounds = [part, swap(part, n_doc // 2)]
    *relayed, far = merge(queue, len(far_zs), n_y, *far_state)
    relayed = [swap(v, 2 * n_doc * (dz - n_z // 2)) for v, dz in zip(relayed, far_zs)]
    mid_state = do_join(mid_zs, mid_state)
    far = swap(total(queue, [far, *relayed]), n_doc * n_z)
    near_state = do_join((0,), near_state)
    sends = merge(queue, len(mid_zs), n_y, *mid_state)
    last = [swap(v, 2 * n_doc * dz) for v, dz in zip(sends, mid_zs)]
    near, = merge(queue, 1, n_y, *near_state)
    rows, inv = inverse(queue, rounds)
    return finish(queue, near, [far, *last], rows, inv)


def solution(mesh):
    in_specs = (P(("term", "doc"), None, None), P(("term", "doc"), None), P("doc", None), P())
    out_specs = (P(("term", "doc"), None), P(("term", "doc"), None))
    run = functools.partial(body, mesh.shape["term"], mesh.shape["doc"])
    return jax.shard_map(run, mesh=mesh, in_specs=in_specs, out_specs=out_specs, check_vma=False)
```

```python
import functools

import jax
import jax.numpy as jnp
from jax import lax
from jax.experimental import pallas as pl
from jax.experimental.pallas import tpu as pltpu
from jax.sharding import PartitionSpec as P

ROWS_DEV = 256
UNROLL = 16
FETCHES = 4
AWAY_MIB = 32
HERE_MIB = 24
F32 = jnp.float32
BF16 = jnp.bfloat16
AXES = ("term", "doc")
TOKEN = (8, 128)
LIMIT = pltpu.CompilerParams(vmem_limit_bytes=24 * 2**20)
LARGE = pltpu.CompilerParams(vmem_limit_bytes=32 * 2**20)
TINY = pl.CostEstimate(flops=1, bytes_accessed=1, transcendentals=0)
ANY = pl.BlockSpec(memory_space=pl.ANY)
HBM = pl.BlockSpec(memory_space=pltpu.HBM)
SMEM = pl.BlockSpec(memory_space=pltpu.SMEM)
VMEM = pl.BlockSpec(memory_space=pltpu.VMEM)


def shaped(shape, dtype=F32):
    return jax.ShapeDtypeStruct(tuple(shape), dtype)


def split(v):
    hi = v.astype(BF16)
    lo = (v - hi.astype(F32)).astype(BF16)
    return hi, lo


def hdot(a, b, dims):
    return lax.dot_general(a, b, (dims, ((), ())), precision=lax.Precision.HIGHEST, preferred_element_type=F32)


def in_order(kernel, last, _token, *refs):
    kernel(*refs[:last], *refs[last + 1 :])
    refs[last][...] = jnp.zeros_like(refs[last])


class Queue:
    def __init__(self, token):
        self.token = token

    def call(self, name, kernel, out_shape, args, smem=()):
        got = pl.pallas_call(
            functools.partial(in_order, kernel, len(args) + len(smem)),
            out_shape=(shaped(TOKEN),) + tuple(out_shape),
            in_specs=[VMEM] * (1 + len(args)) + [SMEM] * len(smem),
            out_specs=(VMEM,) * (1 + len(out_shape)),
            compiler_params=LIMIT,
            cost_estimate=TINY,
            name=name,
        )(self.token, *args, *smem)
        self.token = got[0]
        return got[1:]


def products_kernel(slots, away, code_ref, *refs):
    if away:
        tiles_in, g_ref, blocks, token, tiles, top_ref, low_ref, order, flag, in_sem = refs
    else:
        tiles, top_ref, low_ref, blocks, token, order, flag = refs
    n_tiles, tile = tiles.shape[:2]
    width = top_ref.shape[1]
    share = n_tiles // FETCHES
    spans = [pl.ds(q * share, share) for q in range(FETCHES)]
    if away:
        loads = [pltpu.make_async_copy(tiles_in.at[span], tiles.at[span], in_sem.at[q]) for q, span in enumerate(spans)]
        for load in loads:
            load.start()
    token[...] = jnp.zeros_like(token)

    def scan(k, count):
        code = code_ref[k]
        order[count] = code | (k << 16)
        return count + (((code >> 10) & 1) == away).astype(jnp.int32)

    counts = [jnp.int32(0)]
    for q in range(FETCHES):
        counts.append(lax.fori_loop(q * share, (q + 1) * share, scan, counts[-1], unroll=8))
    blocks[...] = jnp.zeros_like(blocks)
    flag[...] = jnp.zeros_like(flag)
    if away:
        hi, lo = split(g_ref[...])
        top_ref[...] = hi
        low_ref[...] = lo

    def product(code):
        hi, lo = split(tiles[code >> 16])
        rows = pl.ds(pl.multiple_of(((code >> 12) & 15) * tile, tile), tile)
        top = top_ref[rows, :]
        lhs = jnp.concatenate([hi, lo], axis=1)
        both = jnp.dot(lhs, jnp.concatenate([top, top], axis=0), preferred_element_type=F32)
        return both + jnp.dot(hi, low_ref[rows, :], preferred_element_type=F32)

    def several(base, many):
        codes = [order[base + u] for u in range(many)]
        prods = [product(code) for code in codes]
        for code, prod in zip(codes, prods):
            slot = code & 1023
            blocks[slot] += prod
            flag[pl.ds(slot, 1), :] = jnp.full((1, width), ((code >> 11) & 1).astype(F32), F32)

    def group(j, carry):
        several(j * UNROLL, UNROLL)
        return carry

    def single(i, carry):
        several(i, 1)
        return carry

    whole = [count // UNROLL for count in counts]
    if away:
        for q in range(FETCHES):
            loads[q].wait()
            lax.fori_loop(whole[q], whole[q + 1], group, 0)
    else:
        lax.fori_loop(0, whole[-1], group, 0)
    lax.fori_loop(whole[-1] * UNROLL, counts[-1], single, 0)
    blocks[slots, pl.ds(0, slots), :] = flag[pl.ds(0, slots), :]


def products(slots, away, codes, tiles, *factors):
    n_tiles, tile = tiles.shape[:2]
    rows, width = factors[0].shape
    outs = [shaped((slots + 1, tile, width)), shaped(TOKEN)]
    scratch = [pltpu.SMEM((n_tiles + 8,), jnp.int32), pltpu.VMEM((slots + 8, width), F32)]
    if away:
        outs += [shaped(tiles.shape)] + [shaped((rows, width), BF16)] * 2
        scratch.append(pltpu.SemaphoreType.DMA((FETCHES,)))
    return pl.pallas_call(
        functools.partial(products_kernel, slots, away),
        out_shape=outs,
        in_specs=[SMEM, HBM if away else VMEM] + [VMEM] * len(factors),
        out_specs=[VMEM] * len(outs),
        scratch_shapes=scratch,
        compiler_params=pltpu.CompilerParams(vmem_limit_bytes=(AWAY_MIB if away else HERE_MIB) * 2**20),
        cost_estimate=pl.CostEstimate(flops=8 * 10**9, bytes_accessed=5 * 2**20, transcendentals=0),
        name="products_away" if away else "products_here",
    )(codes, tiles, *factors)


def encode(n_doc, me, block, extra, per):
    rel = lax.bitwise_xor(block // per, me)
    core = (rel // n_doc) & 1
    slot = (rel // (2 * n_doc)) * n_doc + (rel & (n_doc - 1))
    return slot | (core << 10) | ((block % per) << 11) | (extra << 12)


def pick_kernel(n_tiles, away, here, code_ref, out):
    slots = away.shape[0] - 1
    out[...] = jnp.zeros_like(out)

    def take(i, code, ref):
        slot = code & 1023
        value = ref[slot, pl.ds(code >> 12, 1), :]
        same = ref[slots, pl.ds(slot, 1), :] == ((code >> 11) & 1).astype(F32)
        out[pl.ds(i, 1), :] = jnp.where(same, value, 0.0)

    def pick(i, carry):
        code = code_ref[n_tiles + i]
        other = ((code >> 10) & 1) == 1

        @pl.when(other)
        def _():
            take(i, code, away)

        @pl.when(jnp.logical_not(other))
        def _():
            take(i, code, here)

        return carry

    lax.fori_loop(0, out.shape[0], pick, 0, unroll=4)


def encode(n_doc, me, block, extra, per):
    rel = lax.bitwise_xor(block // per, me)
    core = (rel // n_doc) & 1
    slot = (rel // (2 * n_doc)) * n_doc + (rel & (n_doc - 1))
    return slot | (core << 10) | ((block % per) << 11) | (extra << 12)


def spread_kernel(zs, n_y, own, got, stay, send_x, *send_y):
    slots = own.shape[0] - 1
    half = own.shape[1] // 2
    n_x = len(zs) * 2 * n_y
    for i, dz in enumerate(zs):
        for dy in range(n_y):
            for dx in range(2):
                slot = (dz * n_y + dy) * 2 + dx
                a, b = own[slot], got[slot]
                up_a = a * own[slots, pl.ds(slot, 1), :]
                up_b = b * got[slots, pl.ds(slot, 1), :]
                for s, value in enumerate(((a - up_a) + (b - up_b), up_a + up_b)):
                    at = 2 * (i * n_y + dy) + s
                    if dx:
                        send_x[at] = value[:half]
                    else:
                        stay[at] = value[:half]
                    at = 2 * (i * 2 + dx) + s
                    if dy:
                        send_y[dy - 1][at] = value[half:]
                    else:
                        stay[n_x + at] = value[half:]


def spread(queue, zs, n_y, own, got):
    half, width = own.shape[1] // 2, own.shape[2]
    n_x, n_yy = len(zs) * 2 * n_y, len(zs) * 4
    outs = (shaped((n_x + n_yy, half, width)), shaped((n_x, half, width))) + (shaped((n_yy, half, width)),) * (n_y - 1)
    stay, send_x, *send_y = queue.call("spread", functools.partial(spread_kernel, zs, n_y), outs, (own, got))
    return stay, send_x, send_y


def join_kernel(n, n_y, stay, got_x, *refs):
    got_y = refs[: n_y - 1]
    keep, send_x = refs[n_y - 1 : n_y + 1]
    send_y = refs[n_y + 1 :]
    n_x = n * 2 * n_y
    for i in range(n):
        for s in range(2):
            for dy in range(n_y):
                at = 2 * (i * n_y + dy) + s
                value = stay[at] + got_x[at]
                if dy:
                    send_y[dy - 1][2 * i + s] = value
                else:
                    keep[4 * i + s] = value
            for dx in range(2):
                at = 2 * (i * 2 + dx) + s
                value = stay[n_x + at]
                for ref in got_y:
                    value = value + ref[at]
                if dx:
                    send_x[2 * i + s] = value
                else:
                    keep[4 * i + 2 + s] = value


def join(queue, n, n_y, stay, got_x, got_y):
    half, width = stay.shape[1:]
    outs = (shaped((4 * n, half, width)),) + (shaped((2 * n, half, width)),) * n_y
    keep, send_x, *send_y = queue.call("join", functools.partial(join_kernel, n, n_y), outs, (stay, got_x, *got_y))
    return keep, send_x, send_y


def merge_kernel(n, n_y, n_far, keep, got_x, *refs):
    got_y, far, outs = refs[: n_y - 1], refs[n_y - 1 : n_y - 1 + n_far], refs[n_y - 1 + n_far :]
    for i, out in enumerate(outs):
        for s in range(2):
            x = keep[4 * i + s]
            y = keep[4 * i + 2 + s] + got_x[2 * i + s]
            for ref in got_y:
                x = x + ref[2 * i + s]
            if i == n - 1:
                for ref in far:
                    x = x + ref[s]
                    y = y + ref[2 + s]
            out[s] = x
            out[2 + s] = y


def merge(queue, n, n_y, keep, got_x, got_y, far=()):
    outs = (shaped((4,) + keep.shape[1:]),) * n
    return queue.call("merge", functools.partial(merge_kernel, n, n_y, len(far)), outs, (keep, got_x, *got_y, *far))


def total_kernel(*refs):
    total = refs[0][...]
    for ref in refs[1:-1]:
        total = total + ref[...]
    refs[-1][...] = total


def total(queue, values):
    return queue.call("total", total_kernel, (shaped(values[0].shape),), values)[0]


def gram_kernel(n_in, *refs):
    ins, (rows_ref, gram_ref) = refs[:n_in], refs[n_in:]
    rows = ins[0][...]
    for ref in ins[1:]:
        rows = rows + ref[...]
    rows_ref[...] = rows
    count = rows.shape[0]
    gram = hdot(rows, rows, ((1,), (1,)))
    diagonal = lax.broadcasted_iota(jnp.int32, (count, count), 0) == lax.broadcasted_iota(jnp.int32, (count, count), 1)
    ridge = 0.001 * jnp.sum(jnp.where(diagonal, gram, 0.0)) / count
    gram_ref[...] = jnp.where(diagonal, gram + ridge, gram)


def gram_of(queue, parts):
    count, width = parts[0].shape
    return queue.call("gram", functools.partial(gram_kernel, len(parts)), (shaped((count, width)), shaped((count, count))), parts)


def eliminate_kernel(lo, hi, given, out):
    m = given[...]
    count = m.shape[0]
    at_row = lax.broadcasted_iota(jnp.int32, (count, count), 0)
    at_col = lax.broadcasted_iota(jnp.int32, (count, count), 1)
    for k in range(lo, hi):
        row = m[k : k + 1, :]
        col = m[:, k : k + 1]
        scale = 1.0 / m[k : k + 1, k : k + 1]
        row = jnp.where(at_col[:1] == k, 1.0, row) * scale
        m = jnp.where(at_row == k, row, jnp.where(at_col == k, 0.0, m) - col * row)
    out[...] = m


def eliminate(queue, m, part, parts):
    count = m.shape[0]
    lo, hi = count * part // parts, count * (part + 1) // parts
    return queue.call("eliminate", functools.partial(eliminate_kernel, lo, hi), (shaped(m.shape),), (m,))[0]


def finish_kernel(n_far, near, *refs):
    x, y = near[:2], near[2:]
    for ref in refs[:n_far]:
        x = x + ref[:2]
        y = y + ref[2:]
    rows_ref, inv_ref, coef_ref, res_ref = refs[n_far:]
    owned = jnp.concatenate([x[0], y[0], x[1], y[1]], axis=0)
    rows = rows_ref[...]
    project = hdot(rows, owned, ((1,), (1,)))
    coef = hdot(inv_ref[...], project, ((1,), (0,)))
    coef_ref[...] = coef
    res_ref[...] = owned - hdot(coef, rows, ((0,), (0,)))


def finish(queue, near, far, rows, inv):
    half, width = near.shape[1:]
    outs = (shaped((rows.shape[0], 4 * half)), shaped((4 * half, width)))
    coef, res = queue.call("finish", functools.partial(finish_kernel, len(far)), outs, (near, *far, rows, inv))
    return coef.T, res


def body(n_term, n_doc, tiles, coords, sketch, anchors):
    devices = n_term * n_doc
    n_y, n_z = n_doc // 2, n_term // 2
    tile, width = tiles.shape[1], sketch.shape[1]
    per = ROWS_DEV // tile
    me = lax.axis_index(AXES).astype(jnp.int32)
    doc_base = lax.axis_index("doc").astype(jnp.int32) * (sketch.shape[0] // tile)

    def swap(v, mask):
        return lax.ppermute(v, AXES, [(i, i ^ mask) for i in range(devices)])

    def swap_y(values):
        return [swap(v, 2 * (k + 1)) for k, v in enumerate(values)]

    codes = jnp.concatenate([
        encode(n_doc, me, coords[:, 0], coords[:, 1] - doc_base, per),
        encode(n_doc, me, anchors // tile, anchors % tile, per),
    ])
    slots = n_z * n_doc
    away, _, tiles_here, top, low = products(slots, 1, codes, tiles, sketch)
    got = swap(away, n_doc)
    here, token = products(slots, 0, codes, tiles_here, top, low)
    queue = Queue(token)

    def do_spread(zs):
        stay, send_x, send_y = spread(queue, zs, n_y, here, got)
        return stay, swap(send_x, 1), swap_y(send_y)

    def do_join(zs, state):
        keep, send_x, send_y = join(queue, len(zs), n_y, *state)
        return keep, swap(send_x, 1), swap_y(send_y)

    far_zs, mid_zs = tuple(range(n_z - 1, n_z // 2 - 1, -1)), tuple(range(n_z // 2 - 1, 0, -1))
    far_state = do_spread(far_zs)
    pick = functools.partial(pick_kernel, tiles.shape[0])
    part, = queue.call("pick", pick, (shaped((anchors.shape[0], width)),), (away, here), (codes,))
    masks = [n_doc << b for b in range((n_term - 1).bit_length())]
    for mask in masks[:-1]:
        part = total(queue, [part, swap(part, mask)])
    rounds = [part, swap(part, masks[-1])]
    far_state = do_join(far_zs, far_state)
    part = total(queue, rounds)
    rounds = [part, swap(part, 1)]
    mid_state = do_spread(mid_zs)
    near_state = do_spread((0,))
    *relayed, far = merge(queue, len(far_zs), n_y, *far_state)
    relayed = [swap(v, 2 * n_doc * (dz - n_z // 2)) for v, dz in zip(relayed, far_zs)]
    part = total(queue, rounds)
    for b in range(1, (n_doc - 1).bit_length() - 1):
        part = total(queue, [part, swap(part, 1 << b)])
    rounds = [part, swap(part, n_doc // 2)]
    mid_state = do_join(mid_zs, mid_state)
    far = swap(total(queue, [far, *relayed]), n_doc * n_z)
    near_state = do_join((0,), near_state)
    rows, gram = gram_of(queue, rounds)
    gram = eliminate(queue, gram, 0, 4)
    sends = merge(queue, len(mid_zs), n_y, *mid_state)
    last = [swap(v, 2 * n_doc * dz) for v, dz in zip(sends, mid_zs)]
    gram = eliminate(queue, gram, 1, 4)
    near, = merge(queue, 1, n_y, *near_state)
    for p in range(2, 4):
        gram = eliminate(queue, gram, p, 4)
    return finish(queue, near, [far, *last], rows, gram)


def solution(mesh):
    in_specs = (P(("term", "doc"), None, None), P(("term", "doc"), None), P("doc", None), P())
    out_specs = (P(("term", "doc"), None), P(("term", "doc"), None))
    run = functools.partial(body, mesh.shape["term"], mesh.shape["doc"])
    return jax.shard_map(run, mesh=mesh, in_specs=in_specs, out_specs=out_specs, check_vma=False)
```

```python
import functools

import jax
import jax.numpy as jnp
from jax import lax
from jax.experimental import pallas as pl
from jax.experimental.pallas import tpu as pltpu
from jax.sharding import PartitionSpec as P

ROWS_DEV = 256
UNROLL = 16
FETCHES = 8
AWAY_MIB = 32
HERE_MIB = 24
F32 = jnp.float32
BF16 = jnp.bfloat16
AXES = ("term", "doc")
TOKEN = (8, 128)
LIMIT = pltpu.CompilerParams(vmem_limit_bytes=24 * 2**20)
LARGE = pltpu.CompilerParams(vmem_limit_bytes=32 * 2**20)
TINY = pl.CostEstimate(flops=1, bytes_accessed=1, transcendentals=0)
LONG = pl.CostEstimate(flops=4 * 10**9, bytes_accessed=1, transcendentals=0)
ANY = pl.BlockSpec(memory_space=pl.ANY)
HBM = pl.BlockSpec(memory_space=pltpu.HBM)
SMEM = pl.BlockSpec(memory_space=pltpu.SMEM)
VMEM = pl.BlockSpec(memory_space=pltpu.VMEM)


def shaped(shape, dtype=F32):
    return jax.ShapeDtypeStruct(tuple(shape), dtype)


def split(v):
    hi = v.astype(BF16)
    lo = (v - hi.astype(F32)).astype(BF16)
    return hi, lo


def hdot(a, b, dims):
    return lax.dot_general(a, b, (dims, ((), ())), precision=lax.Precision.HIGHEST, preferred_element_type=F32)


def in_order(kernel, last, _token, *refs):
    kernel(*refs[:last], *refs[last + 1 :])
    refs[last][...] = jnp.zeros_like(refs[last])


class Queue:
    def __init__(self, token):
        self.token = token

    def call(self, name, kernel, out_shape, args, smem=(), cost=TINY):
        got = pl.pallas_call(
            functools.partial(in_order, kernel, len(args) + len(smem)),
            out_shape=(shaped(TOKEN),) + tuple(out_shape),
            in_specs=[VMEM] * (1 + len(args)) + [SMEM] * len(smem),
            out_specs=(VMEM,) * (1 + len(out_shape)),
            compiler_params=LIMIT,
            cost_estimate=cost,
            name=name,
        )(self.token, *args, *smem)
        self.token = got[0]
        return got[1:]


def products_kernel(slots, away, code_ref, *refs):
    if away:
        tiles_in, g_ref, blocks, token, tiles, top_ref, low_ref, order, flag, in_sem = refs
    else:
        tiles, top_ref, low_ref, blocks, token, order, flag = refs
    n_tiles, tile = tiles.shape[:2]
    width = top_ref.shape[1]
    share = n_tiles // FETCHES
    spans = [pl.ds(q * share, share) for q in range(FETCHES)]
    if away:
        loads = [pltpu.make_async_copy(tiles_in.at[span], tiles.at[span], in_sem.at[q]) for q, span in enumerate(spans)]
        for load in loads:
            load.start()
    token[...] = jnp.zeros_like(token)

    def scan(k, count):
        code = code_ref[k]
        order[count] = code | (k << 16)
        return count + (((code >> 10) & 1) == away).astype(jnp.int32)

    counts = [jnp.int32(0)]
    for q in range(FETCHES):
        counts.append(lax.fori_loop(q * share, (q + 1) * share, scan, counts[-1], unroll=8))
    for u in range(UNROLL):
        order[counts[-1] + u] = slots
    blocks[...] = jnp.zeros_like(blocks)
    flag[...] = jnp.zeros_like(flag)
    if away:
        hi, lo = split(g_ref[...])
        top_ref[...] = hi
        low_ref[...] = lo

    def product(code):
        hi, lo = split(tiles[code >> 16])
        rows = pl.ds(pl.multiple_of(((code >> 12) & 15) * tile, tile), tile)
        top = top_ref[rows, :]
        lhs = jnp.concatenate([hi, lo], axis=1)
        both = jnp.dot(lhs, jnp.concatenate([top, top], axis=0), preferred_element_type=F32)
        return both + jnp.dot(hi, low_ref[rows, :], preferred_element_type=F32)

    def several(base, many):
        codes = [order[base + u] for u in range(many)]
        prods = [product(code) for code in codes]
        for code, prod in zip(codes, prods):
            slot = code & 1023
            blocks[slot] += prod
            flag[pl.ds(slot, 1), :] = jnp.full((1, width), ((code >> 11) & 1).astype(F32), F32)

    def group(j, carry):
        several(j * UNROLL, UNROLL)
        return carry

    whole = [count // UNROLL for count in counts[:-1]] + [(counts[-1] + UNROLL - 1) // UNROLL]
    if away:
        for q in range(FETCHES):
            loads[q].wait()
            lax.fori_loop(whole[q], whole[q + 1], group, 0)
    else:
        lax.fori_loop(0, whole[-1], group, 0)
    blocks[slots, pl.ds(0, slots), :] = flag[pl.ds(0, slots), :]


def products(slots, away, codes, tiles, *factors):
    n_tiles, tile = tiles.shape[:2]
    rows, width = factors[0].shape
    outs = [shaped((slots + 1, tile, width)), shaped(TOKEN)]
    scratch = [pltpu.SMEM((n_tiles + UNROLL,), jnp.int32), pltpu.VMEM((slots + 8, width), F32)]
    if away:
        outs += [shaped(tiles.shape)] + [shaped((rows, width), BF16)] * 2
        scratch.append(pltpu.SemaphoreType.DMA((FETCHES,)))
    return pl.pallas_call(
        functools.partial(products_kernel, slots, away),
        out_shape=outs,
        in_specs=[SMEM, HBM if away else VMEM] + [VMEM] * len(factors),
        out_specs=[VMEM] * len(outs),
        scratch_shapes=scratch,
        compiler_params=pltpu.CompilerParams(vmem_limit_bytes=(AWAY_MIB if away else HERE_MIB) * 2**20),
        cost_estimate=pl.CostEstimate(flops=8 * 10**9, bytes_accessed=5 * 2**20, transcendentals=0),
        name="products_away" if away else "products_here",
    )(codes, tiles, *factors)


def encode(n_doc, me, block, per):
    rel = lax.bitwise_xor(block // per, me)
    core = (rel // n_doc) & 1
    slot = (rel // (2 * n_doc)) * n_doc + (rel & (n_doc - 1))
    return slot | (core << 10) | ((block % per) << 11)


def pick_kernel(n_tiles, away, here, code_ref, out):
    slots = away.shape[0] - 1
    for i in range(out.shape[0]):
        code = code_ref[n_tiles + i]
        slot, row = code & 1023, code >> 12
        bit = ((code >> 11) & 1).astype(F32)
        other = ((code >> 10) & 1) == 1
        value = jnp.where(other, away[slot, pl.ds(row, 1), :], here[slot, pl.ds(row, 1), :])
        which = jnp.where(other, away[slots, pl.ds(slot, 1), :], here[slots, pl.ds(slot, 1), :])
        out[i : i + 1, :] = jnp.where(which == bit, value, 0.0)


def spread_kernel(groups, n_y, own, got, stay, *sends):
    slots = own.shape[0] - 1
    half = own.shape[1] // 2
    n_x = sum(len(zs) for zs in groups) * 2 * n_y
    i = 0
    for g, zs in enumerate(groups):
        send_x, *send_y = sends[g * n_y : (g + 1) * n_y]
        for j, dz in enumerate(zs):
            for dy in range(n_y):
                for dx in range(2):
                    slot = (dz * n_y + dy) * 2 + dx
                    a, b = own[slot], got[slot]
                    up_a = a * own[slots, pl.ds(slot, 1), :]
                    up_b = b * got[slots, pl.ds(slot, 1), :]
                    for s, value in enumerate(((a - up_a) + (b - up_b), up_a + up_b)):
                        if dx:
                            send_x[2 * (j * n_y + dy) + s] = value[:half]
                        else:
                            stay[2 * (i * n_y + dy) + s] = value[:half]
                        if dy:
                            send_y[dy - 1][2 * (j * 2 + dx) + s] = value[half:]
                        else:
                            stay[n_x + 2 * (i * 2 + dx) + s] = value[half:]
            i += 1


def spread(queue, groups, n_y, own, got):
    half, width = own.shape[1] // 2, own.shape[2]
    n = sum(len(zs) for zs in groups)
    outs = [shaped((n * (2 * n_y + 4), half, width))]
    for zs in groups:
        outs += [shaped((len(zs) * 2 * n_y, half, width))] + [shaped((len(zs) * 4, half, width))] * (n_y - 1)
    return queue.call("spread", functools.partial(spread_kernel, groups, n_y), outs, (own, got))


def join_kernel(groups, n_y, n_parts, ride_x, stay, *refs):
    n = sum(len(zs) for zs in groups)
    came = refs[: len(groups) * n_y]
    parts = refs[len(came) : len(came) + n_parts]
    keep, rows, send_x, *send_y = refs[len(came) + n_parts :]
    n_x = n * 2 * n_y
    i = 0
    for g, zs in enumerate(groups):
        got_x, *got_y = came[g * n_y : (g + 1) * n_y]
        for j in range(len(zs)):
            for s in range(2):
                for dy in range(n_y):
                    value = stay[2 * (i * n_y + dy) + s] + got_x[2 * (j * n_y + dy) + s]
                    if dy:
                        send_y[dy - 1][2 * i + s] = value
                    else:
                        keep[4 * i + s] = value
                for dx in range(2):
                    value = stay[n_x + 2 * (i * 2 + dx) + s]
                    for ref in got_y:
                        value = value + ref[2 * (j * 2 + dx) + s]
                    if dx:
                        send_x[2 * i + s] = value
                    else:
                        keep[4 * i + 2 + s] = value
            i += 1
    total = parts[0][...]
    for ref in parts[1:]:
        total = total + ref[...]
    rows[...] = total
    for ref in [send_x] if ride_x else send_y:
        ref[2 * n] = total


def join(queue, groups, n_y, state, parts, ride_x):
    stay = state[0]
    half, width = stay.shape[1:]
    n = sum(len(zs) for zs in groups)
    pairs = [shaped((2 * n + (1 if ride_x == (k == 0) else 0), half, width)) for k in range(n_y)]
    outs = [shaped((4 * n, half, width)), shaped((half, width))] + pairs
    kernel = functools.partial(join_kernel, groups, n_y, len(parts), ride_x)
    return queue.call("join", kernel, outs, (*state, *parts))


def merge_kernel(n, n_y, ride_x, keep, rows, got_x, *refs):
    got_y, total, outs = refs[: n_y - 1], refs[n_y - 1], refs[n_y:]
    for i, out in enumerate(outs):
        for s in range(2):
            x = keep[4 * i + s]
            for ref in got_y:
                x = x + ref[2 * i + s]
            out[s] = x
            out[2 + s] = keep[4 * i + 2 + s] + got_x[2 * i + s]
    value = rows[...]
    for ref in [got_x] if ride_x else got_y:
        value = value + ref[2 * n]
    total[...] = value


def merge(queue, n, n_y, keep, rows, came, ride_x):
    outs = (shaped(rows.shape),) + (shaped((4,) + keep.shape[1:]),) * n
    return queue.call("merge", functools.partial(merge_kernel, n, n_y, ride_x), outs, (keep, rows, *came))


def total_kernel(*refs):
    total = refs[0][...]
    for ref in refs[1:-1]:
        total = total + ref[...]
    refs[-1][...] = total


def total(queue, values):
    return queue.call("total", total_kernel, (shaped(values[0].shape),), values)[0]


def gram_kernel(rows_ref, gram_ref):
    rows = rows_ref[...]
    count = rows.shape[0]
    gram = hdot(rows, rows, ((1,), (1,)))
    diagonal = lax.broadcasted_iota(jnp.int32, (count, count), 0) == lax.broadcasted_iota(jnp.int32, (count, count), 1)
    ridge = 0.001 * jnp.sum(jnp.where(diagonal, gram, 0.0)) / count
    gram_ref[...] = jnp.where(diagonal, gram + ridge, gram)


def gram_of(queue, rows):
    return queue.call("gram", gram_kernel, (shaped((rows.shape[0],) * 2),), (rows,))[0]


def eliminate_kernel(lo, hi, given, out):
    m = given[...]
    count = m.shape[0]
    at_row = lax.broadcasted_iota(jnp.int32, (count, count), 0)
    at_col = lax.broadcasted_iota(jnp.int32, (count, count), 1)
    for k in range(lo, hi):
        row = m[k : k + 1, :]
        col = m[:, k : k + 1]
        scale = 1.0 / m[k : k + 1, k : k + 1]
        row = jnp.where(at_col[:1] == k, 1.0, row) * scale
        m = jnp.where(at_row == k, row, jnp.where(at_col == k, 0.0, m) - col * row)
    out[...] = m


def eliminate(queue, m, part, cost):
    half = m.shape[0] // 2
    kernel = functools.partial(eliminate_kernel, part * half, (part + 1) * half)
    return queue.call("eliminate", kernel, (shaped(m.shape),), (m,), cost=cost)[0]


def solver_kernel(rows, inv, out):
    out[...] = hdot(rows[...], inv[...], ((0,), (0,)))


def solver(queue, rows, inv):
    return queue.call("solver", solver_kernel, (shaped(rows.shape[::-1]),), (rows, inv))[0]


def finish_kernel(n_far, near, *refs):
    x, y = near[:2], near[2:]
    for ref in refs[:n_far]:
        x = x + ref[:2]
        y = y + ref[2:]
    rows_ref, solve_ref, coef_ref, res_ref = refs[n_far:]
    owned = jnp.concatenate([x[0], y[0], x[1], y[1]], axis=0)
    coef = hdot(owned, solve_ref[...], ((1,), (0,)))
    res_ref[...] = owned - hdot(coef, rows_ref[...], ((1,), (0,)))
    coef_ref[...] = coef.T


def finish(queue, near, far, rows, solve):
    half, width = near.shape[1:]
    outs = (shaped((rows.shape[0], 4 * half)), shaped((4 * half, width)))
    coef, res = queue.call("finish", functools.partial(finish_kernel, len(far)), outs, (near, *far, rows, solve))
    return coef.T, res


def body(n_term, n_doc, tiles, coords, sketch, anchors):
    devices = n_term * n_doc
    n_y, n_z = n_doc // 2, n_term // 2
    tile, width = tiles.shape[1], sketch.shape[1]
    per = ROWS_DEV // tile
    me = lax.axis_index(AXES).astype(jnp.int32)
    doc_base = lax.axis_index("doc").astype(jnp.int32) * (sketch.shape[0] // tile)

    def swap(v, mask):
        return lax.ppermute(v, AXES, [(i, i ^ mask) for i in range(devices)])

    def swap_y(values):
        return [swap(v, 2 * (k + 1)) for k, v in enumerate(values)]

    n_tiles, count = coords.shape[0], anchors.shape[0]
    is_block = lax.broadcasted_iota(jnp.int32, (2, n_tiles + count), 0) == 0
    anchor = jnp.where(is_block[:, :count], anchors // tile, anchors % tile + doc_base)
    pair = jnp.pad(coords.T, ((0, 0), (0, count))) + jnp.pad(anchor, ((0, 0), (n_tiles, 0)))
    codes = jnp.sum(jnp.where(is_block, encode(n_doc, me, pair, per), (pair - doc_base) << 12), axis=0)
    slots = n_z * n_doc
    away, _, tiles_here, top, low = products(slots, 1, codes, tiles, sketch)
    got = swap(away, n_doc)
    here, token = products(slots, 0, codes, tiles_here, top, low)
    queue = Queue(token)

    def swaps(values):
        return [swap(v, 2 * k if k else 1) for k, v in enumerate(values)]

    def do_spread(groups):
        stay, *sends = spread(queue, groups, n_y, here, got)
        came = []
        for g in range(len(groups)):
            came += swaps(sends[g * n_y : (g + 1) * n_y])
        return [stay, *came]

    def do_join(groups, state, parts, ride_x):
        keep, rows, *sends = join(queue, groups, n_y, state, parts, ride_x)
        return keep, rows, swaps(sends)

    mid = tuple(range(n_z // 2 - 1, 0, -1))
    far_groups = (tuple(range(n_z - 1, n_z // 2 - 1, -1)),)
    near_groups = (mid + (0,),)
    state = do_spread(far_groups)
    pick = functools.partial(pick_kernel, n_tiles)
    part, = queue.call("pick", pick, (shaped((count, width)),), (away, here), (codes,))
    masks = [n_doc << b for b in range((n_term - 1).bit_length())]
    for mask in masks[:-1]:
        part = total(queue, [part, swap(part, mask)])
    joined = do_join(far_groups, state, (part, swap(part, masks[-1])), True)
    state = do_spread(near_groups)
    rows, *relayed, far = merge(queue, len(far_groups[0]), n_y, *joined, True)
    relayed = [swap(v, 2 * n_doc * (dz - n_z // 2)) for v, dz in zip(relayed, far_groups[0])]
    far = swap(total(queue, [far, *relayed]), n_doc * n_z)
    joined = do_join(near_groups, state, (rows,), False)
    rows, *sends, near = merge(queue, len(mid) + 1, n_y, *joined, False)
    last = [swap(v, 2 * n_doc * dz) for v, dz in zip(sends, mid)]
    gram = gram_of(queue, rows)
    gram = eliminate(queue, gram, 0, TINY)
    near = total(queue, [near, far])
    gram = eliminate(queue, gram, 1, LONG)
    solve = solver(queue, rows, gram)
    return finish(queue, near, last, rows, solve)


def solution(mesh):
    in_specs = (P(("term", "doc"), None, None), P(("term", "doc"), None), P("doc", None), P())
    out_specs = (P(("term", "doc"), None), P(("term", "doc"), None))
    run = functools.partial(body, mesh.shape["term"], mesh.shape["doc"])
    return jax.shard_map(run, mesh=mesh, in_specs=in_specs, out_specs=out_specs, check_vma=False)
```

```python
import functools

import jax
import jax.numpy as jnp
from jax import lax
from jax.experimental import pallas as pl
from jax.experimental.pallas import tpu as pltpu
from jax.sharding import PartitionSpec as P

ROWS_DEV = 256
UNROLL = 16
FETCHES = 8
AWAY_MIB = 32
HERE_MIB = 24
F32 = jnp.float32
BF16 = jnp.bfloat16
AXES = ("term", "doc")
TOKEN = (8, 128)
LIMIT = pltpu.CompilerParams(vmem_limit_bytes=24 * 2**20)
LARGE = pltpu.CompilerParams(vmem_limit_bytes=32 * 2**20)
TINY = pl.CostEstimate(flops=1, bytes_accessed=1, transcendentals=0)
LONG = pl.CostEstimate(flops=4 * 10**9, bytes_accessed=1, transcendentals=0)
ANY = pl.BlockSpec(memory_space=pl.ANY)
HBM = pl.BlockSpec(memory_space=pltpu.HBM)
SMEM = pl.BlockSpec(memory_space=pltpu.SMEM)
VMEM = pl.BlockSpec(memory_space=pltpu.VMEM)


def shaped(shape, dtype=F32):
    return jax.ShapeDtypeStruct(tuple(shape), dtype)


def split(v):
    hi = v.astype(BF16)
    lo = (v - hi.astype(F32)).astype(BF16)
    return hi, lo


def hdot(a, b, dims):
    return lax.dot_general(a, b, (dims, ((), ())), precision=lax.Precision.HIGHEST, preferred_element_type=F32)


def in_order(kernel, last, _token, *refs):
    kernel(*refs[:last], *refs[last + 1 :])
    refs[last][...] = jnp.zeros_like(refs[last])


class Queue:
    def __init__(self, token):
        self.token = token

    def call(self, name, kernel, out_shape, args, smem=(), cost=TINY):
        got = pl.pallas_call(
            functools.partial(in_order, kernel, len(args) + len(smem)),
            out_shape=(shaped(TOKEN),) + tuple(out_shape),
            in_specs=[VMEM] * (1 + len(args)) + [SMEM] * len(smem),
            out_specs=(VMEM,) * (1 + len(out_shape)),
            compiler_params=LIMIT,
            cost_estimate=cost,
            name=name,
        )(self.token, *args, *smem)
        self.token = got[0]
        return got[1:]


def products_kernel(slots, away, code_ref, *refs):
    if away:
        tiles_in, g_ref, blocks, token, tiles, top_ref, low_ref, order, flag, in_sem = refs
    else:
        tiles, top_ref, low_ref, blocks, token, order, flag = refs
    n_tiles, tile = tiles.shape[:2]
    width = top_ref.shape[1]
    share = n_tiles // FETCHES
    spans = [pl.ds(q * share, share) for q in range(FETCHES)]
    if away:
        loads = [pltpu.make_async_copy(tiles_in.at[span], tiles.at[span], in_sem.at[q]) for q, span in enumerate(spans)]
        for load in loads:
            load.start()
    token[...] = jnp.zeros_like(token)

    def scan(k, count):
        code = code_ref[k]
        order[count] = code | (k << 16)
        return count + (((code >> 10) & 1) == away).astype(jnp.int32)

    counts = [jnp.int32(0)]
    for q in range(FETCHES):
        counts.append(lax.fori_loop(q * share, (q + 1) * share, scan, counts[-1], unroll=8))
    for u in range(UNROLL):
        order[counts[-1] + u] = slots
    blocks[...] = jnp.zeros_like(blocks)
    flag[...] = jnp.zeros_like(flag)
    if away:
        hi, lo = split(g_ref[...])
        top_ref[...] = hi
        low_ref[...] = lo

    def product(code):
        hi, lo = split(tiles[code >> 16])
        rows = pl.ds(pl.multiple_of(((code >> 12) & 15) * tile, tile), tile)
        top = top_ref[rows, :]
        lhs = jnp.concatenate([hi, lo], axis=1)
        both = jnp.dot(lhs, jnp.concatenate([top, top], axis=0), preferred_element_type=F32)
        return both + jnp.dot(hi, low_ref[rows, :], preferred_element_type=F32)

    def several(base, many):
        codes = [order[base + u] for u in range(many)]
        prods = [product(code) for code in codes]
        for code, prod in zip(codes, prods):
            slot = code & 1023
            blocks[slot] += prod
            flag[pl.ds(slot, 1), :] = jnp.full((1, width), ((code >> 11) & 1).astype(F32), F32)

    def group(j, carry):
        several(j * UNROLL, UNROLL)
        return carry

    whole = [count // UNROLL for count in counts[:-1]] + [(counts[-1] + UNROLL - 1) // UNROLL]
    if away:
        for q in range(FETCHES):
            loads[q].wait()
            lax.fori_loop(whole[q], whole[q + 1], group, 0)
    else:
        lax.fori_loop(0, whole[-1], group, 0)
    blocks[slots, pl.ds(0, slots), :] = flag[pl.ds(0, slots), :]


def products(slots, away, codes, tiles, *factors):
    n_tiles, tile = tiles.shape[:2]
    rows, width = factors[0].shape
    outs = [shaped((slots + 1, tile, width)), shaped(TOKEN)]
    scratch = [pltpu.SMEM((n_tiles + UNROLL,), jnp.int32), pltpu.VMEM((slots + 8, width), F32)]
    if away:
        outs += [shaped(tiles.shape)] + [shaped((rows, width), BF16)] * 2
        scratch.append(pltpu.SemaphoreType.DMA((FETCHES,)))
    return pl.pallas_call(
        functools.partial(products_kernel, slots, away),
        out_shape=outs,
        in_specs=[SMEM, HBM if away else VMEM] + [VMEM] * len(factors),
        out_specs=[VMEM] * len(outs),
        scratch_shapes=scratch,
        compiler_params=pltpu.CompilerParams(vmem_limit_bytes=(AWAY_MIB if away else HERE_MIB) * 2**20),
        cost_estimate=pl.CostEstimate(flops=8 * 10**9, bytes_accessed=5 * 2**20, transcendentals=0),
        name="products_away" if away else "products_here",
    )(codes, tiles, *factors)


def encode(n_doc, me, block, per):
    rel = lax.bitwise_xor(block // per, me)
    core = (rel // n_doc) & 1
    slot = (rel // (2 * n_doc)) * n_doc + (rel & (n_doc - 1))
    return slot | (core << 10) | ((block % per) << 11)


def pick_kernel(n_tiles, away, here, code_ref, out):
    slots = away.shape[0] - 1
    for i in range(out.shape[0]):
        code = code_ref[n_tiles + i]
        slot, row = code & 1023, code >> 12
        bit = ((code >> 11) & 1).astype(F32)
        other = ((code >> 10) & 1) == 1
        value = jnp.where(other, away[slot, pl.ds(row, 1), :], here[slot, pl.ds(row, 1), :])
        which = jnp.where(other, away[slots, pl.ds(slot, 1), :], here[slots, pl.ds(slot, 1), :])
        out[i : i + 1, :] = jnp.where(which == bit, value, 0.0)


def spread_kernel(groups, n_y, own, got, stay, *sends):
    slots = own.shape[0] - 1
    half = own.shape[1] // 2
    n_x = sum(len(zs) for zs in groups) * 2 * n_y
    i = 0
    for g, zs in enumerate(groups):
        send_x, *send_y = sends[g * n_y : (g + 1) * n_y]
        for j, dz in enumerate(zs):
            for dy in range(n_y):
                for dx in range(2):
                    slot = (dz * n_y + dy) * 2 + dx
                    a, b = own[slot], got[slot]
                    up_a = a * own[slots, pl.ds(slot, 1), :]
                    up_b = b * got[slots, pl.ds(slot, 1), :]
                    for s, value in enumerate(((a - up_a) + (b - up_b), up_a + up_b)):
                        if dx:
                            send_x[2 * (j * n_y + dy) + s] = value[:half]
                        else:
                            stay[2 * (i * n_y + dy) + s] = value[:half]
                        if dy:
                            send_y[dy - 1][2 * (j * 2 + dx) + s] = value[half:]
                        else:
                            stay[n_x + 2 * (i * 2 + dx) + s] = value[half:]
            i += 1


def spread(queue, groups, n_y, own, got):
    half, width = own.shape[1] // 2, own.shape[2]
    n = sum(len(zs) for zs in groups)
    outs = [shaped((n * (2 * n_y + 4), half, width))]
    for zs in groups:
        outs += [shaped((len(zs) * 2 * n_y, half, width))] + [shaped((len(zs) * 4, half, width))] * (n_y - 1)
    return queue.call("spread", functools.partial(spread_kernel, groups, n_y), outs, (own, got))


def join_kernel(groups, n_y, n_parts, ride_x, cuts, stay, *refs):
    n = sum(len(zs) for zs in groups)
    came = refs[: len(groups) * n_y]
    parts = refs[len(came) : len(came) + n_parts]
    keep, rows, *sends = refs[len(came) + n_parts :]
    at = [(c, m) for c, cut in enumerate(cuts) for m in range(cut)]
    n_x = n * 2 * n_y
    i = 0
    for g, zs in enumerate(groups):
        got_x, *got_y = came[g * n_y : (g + 1) * n_y]
        for j in range(len(zs)):
            cut, m = at[i]
            send_x, *send_y = sends[cut * n_y : (cut + 1) * n_y]
            for s in range(2):
                for dy in range(n_y):
                    value = stay[2 * (i * n_y + dy) + s] + got_x[2 * (j * n_y + dy) + s]
                    if dy:
                        send_y[dy - 1][2 * m + s] = value
                    else:
                        keep[4 * i + s] = value
                for dx in range(2):
                    value = stay[n_x + 2 * (i * 2 + dx) + s]
                    for ref in got_y:
                        value = value + ref[2 * (j * 2 + dx) + s]
                    if dx:
                        send_x[2 * m + s] = value
                    else:
                        keep[4 * i + 2 + s] = value
            i += 1
    total = parts[0][...]
    for ref in parts[1:]:
        total = total + ref[...]
    rows[...] = total
    for ref in sends[:1] if ride_x else sends[1:n_y]:
        ref[2 * cuts[0]] = total


def join(queue, groups, n_y, state, parts, ride_x, cuts):
    stay = state[0]
    half, width = stay.shape[1:]
    n = sum(len(zs) for zs in groups)
    outs = [shaped((4 * n, half, width)), shaped((half, width))]
    for c, cut in enumerate(cuts):
        outs += [shaped((2 * cut + (1 if c == 0 and ride_x == (k == 0) else 0), half, width)) for k in range(n_y)]
    kernel = functools.partial(join_kernel, groups, n_y, len(parts), ride_x, cuts)
    return queue.call("join", kernel, outs, (*state, *parts))


def merge_kernel(start, n, n_y, ride, keep, got_x, *refs):
    got_y, refs = refs[: n_y - 1], refs[n_y - 1 :]
    if ride is None:
        far, outs = refs[:-n], refs[-n:]
    else:
        far, (rows, total, *outs) = (), refs
        value = rows[...]
        for ref in [got_x] if ride else got_y:
            value = value + ref[2 * n]
        total[...] = value
    for i, out in enumerate(outs):
        for s in range(2):
            x = keep[4 * (start + i) + s]
            y = keep[4 * (start + i) + 2 + s] + got_x[2 * i + s]
            for ref in got_y:
                x = x + ref[2 * i + s]
            for ref in far:
                x = x + ref[s]
                y = y + ref[2 + s]
            out[s] = x
            out[2 + s] = y


def merge(queue, start, n, n_y, keep, came, ride, more):
    outs = (shaped((4,) + keep.shape[1:]),) * n
    if ride is not None:
        outs = (shaped(more[0].shape),) + outs
    return queue.call("merge", functools.partial(merge_kernel, start, n, n_y, ride), outs, (keep, *came, *more))


def total_kernel(*refs):
    total = refs[0][...]
    for ref in refs[1:-1]:
        total = total + ref[...]
    refs[-1][...] = total


def total(queue, values):
    return queue.call("total", total_kernel, (shaped(values[0].shape),), values)[0]


def gram_kernel(rows_ref, gram_ref):
    rows = rows_ref[...]
    count = rows.shape[0]
    gram = hdot(rows, rows, ((1,), (1,)))
    diagonal = lax.broadcasted_iota(jnp.int32, (count, count), 0) == lax.broadcasted_iota(jnp.int32, (count, count), 1)
    ridge = 0.001 * jnp.sum(jnp.where(diagonal, gram, 0.0)) / count
    gram_ref[...] = jnp.where(diagonal, gram + ridge, gram)


def gram_of(queue, rows):
    return queue.call("gram", gram_kernel, (shaped((rows.shape[0],) * 2),), (rows,))[0]


def eliminate_kernel(lo, hi, given, out):
    m = given[...]
    count = m.shape[0]
    at_row = lax.broadcasted_iota(jnp.int32, (count, count), 0)
    at_col = lax.broadcasted_iota(jnp.int32, (count, count), 1)
    for k in range(lo, hi):
        row = m[k : k + 1, :]
        col = m[:, k : k + 1]
        scale = 1.0 / m[k : k + 1, k : k + 1]
        row = jnp.where(at_col[:1] == k, 1.0, row) * scale
        m = jnp.where(at_row == k, row, jnp.where(at_col == k, 0.0, m) - col * row)
    out[...] = m


def eliminate(queue, m, part, cost):
    half = m.shape[0] // 2
    kernel = functools.partial(eliminate_kernel, part * half, (part + 1) * half)
    return queue.call("eliminate", kernel, (shaped(m.shape),), (m,), cost=cost)[0]


def solver_kernel(rows, inv, out):
    out[...] = hdot(rows[...], inv[...], ((0,), (0,)))


def solver(queue, rows, inv):
    return queue.call("solver", solver_kernel, (shaped(rows.shape[::-1]),), (rows, inv))[0]


def finish_kernel(n_far, near, *refs):
    x, y = near[:2], near[2:]
    for ref in refs[:n_far]:
        x = x + ref[:2]
        y = y + ref[2:]
    rows_ref, solve_ref, coef_ref, res_ref = refs[n_far:]
    owned = jnp.concatenate([x[0], y[0], x[1], y[1]], axis=0)
    coef = hdot(owned, solve_ref[...], ((1,), (0,)))
    res_ref[...] = owned - hdot(coef, rows_ref[...], ((1,), (0,)))
    coef_ref[...] = coef.T


def finish(queue, near, far, rows, solve):
    half, width = near.shape[1:]
    outs = (shaped((rows.shape[0], 4 * half)), shaped((4 * half, width)))
    coef, res = queue.call("finish", functools.partial(finish_kernel, len(far)), outs, (near, *far, rows, solve))
    return coef.T, res


def body(n_term, n_doc, tiles, coords, sketch, anchors):
    devices = n_term * n_doc
    n_y, n_z = n_doc // 2, n_term // 2
    tile, width = tiles.shape[1], sketch.shape[1]
    per = ROWS_DEV // tile
    me = lax.axis_index(AXES).astype(jnp.int32)
    doc_base = lax.axis_index("doc").astype(jnp.int32) * (sketch.shape[0] // tile)

    def swap(v, mask):
        return lax.ppermute(v, AXES, [(i, i ^ mask) for i in range(devices)])

    def swap_y(values):
        return [swap(v, 2 * (k + 1)) for k, v in enumerate(values)]

    n_tiles, count = coords.shape[0], anchors.shape[0]
    is_block = lax.broadcasted_iota(jnp.int32, (2, n_tiles + count), 0) == 0
    anchor = jnp.where(is_block[:, :count], anchors // tile, anchors % tile + doc_base)
    pair = jnp.pad(coords.T, ((0, 0), (0, count))) + jnp.pad(anchor, ((0, 0), (n_tiles, 0)))
    codes = jnp.sum(jnp.where(is_block, encode(n_doc, me, pair, per), (pair - doc_base) << 12), axis=0)
    slots = n_z * n_doc
    away, _, tiles_here, top, low = products(slots, 1, codes, tiles, sketch)
    got = swap(away, n_doc)
    here, token = products(slots, 0, codes, tiles_here, top, low)
    queue = Queue(token)

    def swaps(values):
        return [swap(v, 2 * k if k else 1) for k, v in enumerate(values)]

    def do_spread(groups):
        stay, *sends = spread(queue, groups, n_y, here, got)
        came = []
        for g in range(len(groups)):
            came += swaps(sends[g * n_y : (g + 1) * n_y])
        return [stay, *came]

    def do_join(groups, state, parts, ride_x, cuts):
        keep, rows, *sends = join(queue, groups, n_y, state, parts, ride_x, cuts)
        return keep, rows, [swaps(sends[c * n_y : (c + 1) * n_y]) for c in range(len(cuts))]

    mid = tuple(range(n_z // 2 - 1, 0, -1))
    far_groups = (tuple(range(n_z - 1, n_z // 2 - 1, -1)),)
    near_groups = (mid + (0,),)
    state = do_spread(far_groups)
    pick = functools.partial(pick_kernel, n_tiles)
    part, = queue.call("pick", pick, (shaped((count, width)),), (away, here), (codes,))
    masks = [n_doc << b for b in range((n_term - 1).bit_length())]
    for mask in masks[:-1]:
        part = total(queue, [part, swap(part, mask)])
    n_far, n_mid = len(far_groups[0]), len(mid)
    keep, rows, came = do_join(far_groups, state, (part, swap(part, masks[-1])), True, (n_far,))
    state = do_spread(near_groups)
    rows, *relayed, far = merge(queue, 0, n_far, n_y, keep, came[0], True, (rows,))
    relayed = [swap(v, 2 * n_doc * (dz - n_z // 2)) for v, dz in zip(relayed, far_groups[0])]
    far = swap(total(queue, [far, *relayed]), n_doc * n_z)
    keep, rows, came = do_join(near_groups, state, (rows,), False, (n_mid, 1))
    rows, *sends = merge(queue, 0, n_mid, n_y, keep, came[0], False, (rows,))
    last = [swap(v, 2 * n_doc * dz) for v, dz in zip(sends, mid)]
    gram = gram_of(queue, rows)
    gram = eliminate(queue, gram, 0, TINY)
    near, = merge(queue, n_mid, 1, n_y, keep, came[1], None, (far,))
    gram = eliminate(queue, gram, 1, LONG)
    solve = solver(queue, rows, gram)
    return finish(queue, near, last, rows, solve)


def solution(mesh):
    in_specs = (P(("term", "doc"), None, None), P(("term", "doc"), None), P("doc", None), P())
    out_specs = (P(("term", "doc"), None), P(("term", "doc"), None))
    run = functools.partial(body, mesh.shape["term"], mesh.shape["doc"])
    return jax.shard_map(run, mesh=mesh, in_specs=in_specs, out_specs=out_specs, check_vma=False)
```

```python
import functools

import jax
import jax.numpy as jnp
from jax import lax
from jax.experimental import pallas as pl
from jax.experimental.pallas import tpu as pltpu
from jax.sharding import PartitionSpec as P

ROWS_DEV = 256
UNROLL = 16
FETCHES = 8
AWAY_MIB = 32
HERE_MIB = 24
F32 = jnp.float32
BF16 = jnp.bfloat16
AXES = ("term", "doc")
TOKEN = (8, 128)
LIMIT = pltpu.CompilerParams(vmem_limit_bytes=24 * 2**20)
LARGE = pltpu.CompilerParams(vmem_limit_bytes=32 * 2**20)
TINY = pl.CostEstimate(flops=1, bytes_accessed=1, transcendentals=0)
LONG = pl.CostEstimate(flops=4 * 10**9, bytes_accessed=1, transcendentals=0)
ANY = pl.BlockSpec(memory_space=pl.ANY)
HBM = pl.BlockSpec(memory_space=pltpu.HBM)
SMEM = pl.BlockSpec(memory_space=pltpu.SMEM)
VMEM = pl.BlockSpec(memory_space=pltpu.VMEM)


def shaped(shape, dtype=F32):
    return jax.ShapeDtypeStruct(tuple(shape), dtype)


def split(v):
    hi = v.astype(BF16)
    lo = (v - hi.astype(F32)).astype(BF16)
    return hi, lo


def hdot(a, b, dims):
    return lax.dot_general(a, b, (dims, ((), ())), precision=lax.Precision.HIGHEST, preferred_element_type=F32)


def in_order(kernel, last, _token, *refs):
    kernel(*refs[:last], *refs[last + 1 :])
    refs[last][...] = jnp.zeros_like(refs[last])


class Queue:
    def __init__(self, token):
        self.token = token

    def call(self, name, kernel, out_shape, args, smem=(), cost=TINY):
        got = pl.pallas_call(
            functools.partial(in_order, kernel, len(args) + len(smem)),
            out_shape=(shaped(TOKEN),) + tuple(out_shape),
            in_specs=[VMEM] * (1 + len(args)) + [SMEM] * len(smem),
            out_specs=(VMEM,) * (1 + len(out_shape)),
            compiler_params=LIMIT,
            cost_estimate=cost,
            name=name,
        )(self.token, *args, *smem)
        self.token = got[0]
        return got[1:]


def products_kernel(slots, away, code_ref, *refs):
    if away:
        tiles_in, g_ref, blocks, token, tiles, top_ref, low_ref, order, flag, in_sem = refs
    else:
        tiles, top_ref, low_ref, blocks, token, order, flag = refs
    n_tiles, tile = tiles.shape[:2]
    width = top_ref.shape[1]
    share = n_tiles // FETCHES
    spans = [pl.ds(q * share, share) for q in range(FETCHES)]
    if away:
        loads = [pltpu.make_async_copy(tiles_in.at[span], tiles.at[span], in_sem.at[q]) for q, span in enumerate(spans)]
        for load in loads:
            load.start()
    token[...] = jnp.zeros_like(token)

    def scan(k, count):
        code = code_ref[k]
        order[count] = code | (k << 16)
        return count + (((code >> 10) & 1) == away).astype(jnp.int32)

    counts = [jnp.int32(0)]
    for q in range(FETCHES):
        counts.append(lax.fori_loop(q * share, (q + 1) * share, scan, counts[-1], unroll=8))
    for u in range(UNROLL):
        order[counts[-1] + u] = slots
    blocks[...] = jnp.zeros_like(blocks)
    flag[...] = jnp.zeros_like(flag)
    if away:
        hi, lo = split(g_ref[...])
        top_ref[...] = hi
        low_ref[...] = lo

    def product(code):
        hi, lo = split(tiles[code >> 16])
        rows = pl.ds(pl.multiple_of(((code >> 12) & 15) * tile, tile), tile)
        top = top_ref[rows, :]
        lhs = jnp.concatenate([hi, lo], axis=1)
        both = jnp.dot(lhs, jnp.concatenate([top, top], axis=0), preferred_element_type=F32)
        return both + jnp.dot(hi, low_ref[rows, :], preferred_element_type=F32)

    def several(base, many):
        codes = [order[base + u] for u in range(many)]
        prods = [product(code) for code in codes]
        for code, prod in zip(codes, prods):
            slot = code & 1023
            blocks[slot] += prod
            flag[pl.ds(slot, 1), :] = jnp.full((1, width), ((code >> 11) & 1).astype(F32), F32)

    def group(j, carry):
        several(j * UNROLL, UNROLL)
        return carry

    whole = [count // UNROLL for count in counts[:-1]] + [(counts[-1] + UNROLL - 1) // UNROLL]
    if away:
        for q in range(FETCHES):
            loads[q].wait()
            lax.fori_loop(whole[q], whole[q + 1], group, 0)
    else:
        lax.fori_loop(0, whole[-1], group, 0)
    blocks[slots, pl.ds(0, slots), :] = flag[pl.ds(0, slots), :]


def products(slots, away, codes, tiles, *factors):
    n_tiles, tile = tiles.shape[:2]
    rows, width = factors[0].shape
    outs = [shaped((slots + 1, tile, width)), shaped(TOKEN)]
    scratch = [pltpu.SMEM((n_tiles + UNROLL,), jnp.int32), pltpu.VMEM((slots + 8, width), F32)]
    if away:
        outs += [shaped(tiles.shape)] + [shaped((rows, width), BF16)] * 2
        scratch.append(pltpu.SemaphoreType.DMA((FETCHES,)))
    return pl.pallas_call(
        functools.partial(products_kernel, slots, away),
        out_shape=outs,
        in_specs=[SMEM, HBM if away else VMEM] + [VMEM] * len(factors),
        out_specs=[VMEM] * len(outs),
        scratch_shapes=scratch,
        compiler_params=pltpu.CompilerParams(vmem_limit_bytes=(AWAY_MIB if away else HERE_MIB) * 2**20),
        cost_estimate=pl.CostEstimate(flops=8 * 10**9, bytes_accessed=5 * 2**20, transcendentals=0),
        name="products_away" if away else "products_here",
    )(codes, tiles, *factors)


def encode(n_doc, me, block, per):
    rel = lax.bitwise_xor(block // per, me)
    core = (rel // n_doc) & 1
    slot = (rel // (2 * n_doc)) * n_doc + (rel & (n_doc - 1))
    return slot | (core << 10) | ((block % per) << 11)


def pick_kernel(n_tiles, away, here, code_ref, out):
    slots = away.shape[0] - 1
    for i in range(out.shape[0]):
        code = code_ref[n_tiles + i]
        slot, row = code & 1023, code >> 12
        bit = ((code >> 11) & 1).astype(F32)
        other = ((code >> 10) & 1) == 1
        value = jnp.where(other, away[slot, pl.ds(row, 1), :], here[slot, pl.ds(row, 1), :])
        which = jnp.where(other, away[slots, pl.ds(slot, 1), :], here[slots, pl.ds(slot, 1), :])
        out[i : i + 1, :] = jnp.where(which == bit, value, 0.0)


def spread_kernel(groups, n_y, own, got, stay, *sends):
    slots = own.shape[0] - 1
    half = own.shape[1] // 2
    n_x = sum(len(zs) for zs in groups) * 2 * n_y
    i = 0
    for g, zs in enumerate(groups):
        send_x, *send_y = sends[g * n_y : (g + 1) * n_y]
        for j, dz in enumerate(zs):
            for dy in range(n_y):
                for dx in range(2):
                    slot = (dz * n_y + dy) * 2 + dx
                    a, b = own[slot], got[slot]
                    up_a = a * own[slots, pl.ds(slot, 1), :]
                    up_b = b * got[slots, pl.ds(slot, 1), :]
                    for s, value in enumerate(((a - up_a) + (b - up_b), up_a + up_b)):
                        if dx:
                            send_x[2 * (j * n_y + dy) + s] = value[:half]
                        else:
                            stay[2 * (i * n_y + dy) + s] = value[:half]
                        if dy:
                            send_y[dy - 1][2 * (j * 2 + dx) + s] = value[half:]
                        else:
                            stay[n_x + 2 * (i * 2 + dx) + s] = value[half:]
            i += 1


def spread(queue, groups, n_y, own, got):
    half, width = own.shape[1] // 2, own.shape[2]
    n = sum(len(zs) for zs in groups)
    outs = [shaped((n * (2 * n_y + 4), half, width))]
    for zs in groups:
        outs += [shaped((len(zs) * 2 * n_y, half, width))] + [shaped((len(zs) * 4, half, width))] * (n_y - 1)
    return queue.call("spread", functools.partial(spread_kernel, groups, n_y), outs, (own, got))


def join_kernel(groups, n_y, n_parts, ride_x, cuts, stay, *refs):
    n = sum(len(zs) for zs in groups)
    came = refs[: len(groups) * n_y]
    parts = refs[len(came) : len(came) + n_parts]
    keep, rows, *sends = refs[len(came) + n_parts :]
    at = [(c, m) for c, cut in enumerate(cuts) for m in range(cut)]
    n_x = n * 2 * n_y
    i = 0
    for g, zs in enumerate(groups):
        got_x, *got_y = came[g * n_y : (g + 1) * n_y]
        for j in range(len(zs)):
            cut, m = at[i]
            send_x, *send_y = sends[cut * n_y : (cut + 1) * n_y]
            for s in range(2):
                for dy in range(n_y):
                    value = stay[2 * (i * n_y + dy) + s] + got_x[2 * (j * n_y + dy) + s]
                    if dy:
                        send_y[dy - 1][2 * m + s] = value
                    else:
                        keep[4 * i + s] = value
                for dx in range(2):
                    value = stay[n_x + 2 * (i * 2 + dx) + s]
                    for ref in got_y:
                        value = value + ref[2 * (j * 2 + dx) + s]
                    if dx:
                        send_x[2 * m + s] = value
                    else:
                        keep[4 * i + 2 + s] = value
            i += 1
    total = parts[0][...]
    for ref in parts[1:]:
        total = total + ref[...]
    rows[...] = total
    for ref in sends[:1] if ride_x else sends[1:n_y]:
        ref[2 * cuts[0]] = total


def join(queue, groups, n_y, state, parts, ride_x, cuts):
    stay = state[0]
    half, width = stay.shape[1:]
    n = sum(len(zs) for zs in groups)
    outs = [shaped((4 * n, half, width)), shaped((half, width))]
    for c, cut in enumerate(cuts):
        outs += [shaped((2 * cut + (1 if c == 0 and ride_x == (k == 0) else 0), half, width)) for k in range(n_y)]
    kernel = functools.partial(join_kernel, groups, n_y, len(parts), ride_x, cuts)
    return queue.call("join", kernel, outs, (*state, *parts))


def merge_kernel(start, n, n_y, ride, keep, got_x, *refs):
    got_y, refs = refs[: n_y - 1], refs[n_y - 1 :]
    if ride is None:
        far, outs = refs[:-n], refs[-n:]
    else:
        far, (rows, total, *outs) = (), refs
        value = rows[...]
        for ref in [got_x] if ride else got_y:
            value = value + ref[2 * n]
        total[...] = value
    for i, out in enumerate(outs):
        for s in range(2):
            x = keep[4 * (start + i) + s]
            y = keep[4 * (start + i) + 2 + s] + got_x[2 * i + s]
            for ref in got_y:
                x = x + ref[2 * i + s]
            for ref in far:
                x = x + ref[s]
                y = y + ref[2 + s]
            out[s] = x
            out[2 + s] = y


def merge(queue, start, n, n_y, keep, came, ride, more):
    outs = (shaped((4,) + keep.shape[1:]),) * n
    if ride is not None:
        outs = (shaped(more[0].shape),) + outs
    return queue.call("merge", functools.partial(merge_kernel, start, n, n_y, ride), outs, (keep, *came, *more))


def total_kernel(*refs):
    total = refs[0][...]
    for ref in refs[1:-1]:
        total = total + ref[...]
    refs[-1][...] = total


def total(queue, values):
    return queue.call("total", total_kernel, (shaped(values[0].shape),), values)[0]


def gram_kernel(rows_ref, gram_ref):
    rows = rows_ref[...]
    count = rows.shape[0]
    gram = hdot(rows, rows, ((1,), (1,)))
    diagonal = lax.broadcasted_iota(jnp.int32, (count, count), 0) == lax.broadcasted_iota(jnp.int32, (count, count), 1)
    ridge = 0.001 * jnp.sum(jnp.where(diagonal, gram, 0.0)) / count
    gram_ref[...] = jnp.where(diagonal, gram + ridge, gram)


def gram_of(queue, rows):
    return queue.call("gram", gram_kernel, (shaped((rows.shape[0],) * 2),), (rows,))[0]


def eliminate_kernel(lo, hi, given, out):
    m = given[...]
    count = m.shape[0]
    at_row = lax.broadcasted_iota(jnp.int32, (count, count), 0)
    at_col = lax.broadcasted_iota(jnp.int32, (count, count), 1)
    for k in range(lo, hi, 2):
        first, second = m[k : k + 1, :], m[k + 1 : k + 2, :]
        col, next_col = m[:, k : k + 1], m[:, k + 1 : k + 2]
        left = 1.0 / first[:, k : k + 1]
        up = first[:, k + 1 : k + 2] * left
        down = second[:, k : k + 1] * left
        right = 1.0 / (second[:, k + 1 : k + 2] - second[:, k : k + 1] * up)
        place = at_col[:1]
        first = jnp.where(place == k, 1.0, jnp.where(place == k + 1, 0.0, first))
        second = jnp.where(place == k + 1, 1.0, jnp.where(place == k, 0.0, second))
        second = (second - down * first) * right
        first = left * first - up * second
        rest = jnp.where((at_col == k) | (at_col == k + 1), 0.0, m) - col * first - next_col * second
        m = jnp.where(at_row == k, first, jnp.where(at_row == k + 1, second, rest))
    out[...] = m


def eliminate(queue, m, part, cost):
    half = m.shape[0] // 2
    kernel = functools.partial(eliminate_kernel, part * half, (part + 1) * half)
    return queue.call("eliminate", kernel, (shaped(m.shape),), (m,), cost=cost)[0]


def solver_kernel(rows, inv, out):
    out[...] = hdot(rows[...], inv[...], ((0,), (0,)))


def solver(queue, rows, inv):
    return queue.call("solver", solver_kernel, (shaped(rows.shape[::-1]),), (rows, inv))[0]


def finish_kernel(n_far, near, *refs):
    x, y = near[:2], near[2:]
    for ref in refs[:n_far]:
        x = x + ref[:2]
        y = y + ref[2:]
    rows_ref, solve_ref, coef_ref, res_ref = refs[n_far:]
    owned = jnp.concatenate([x[0], y[0], x[1], y[1]], axis=0)
    coef = hdot(owned, solve_ref[...], ((1,), (0,)))
    res_ref[...] = owned - hdot(coef, rows_ref[...], ((1,), (0,)))
    coef_ref[...] = coef.T


def finish(queue, near, far, rows, solve):
    half, width = near.shape[1:]
    outs = (shaped((rows.shape[0], 4 * half)), shaped((4 * half, width)))
    coef, res = queue.call("finish", functools.partial(finish_kernel, len(far)), outs, (near, *far, rows, solve))
    return coef.T, res


def body(n_term, n_doc, tiles, coords, sketch, anchors):
    devices = n_term * n_doc
    n_y, n_z = n_doc // 2, n_term // 2
    tile, width = tiles.shape[1], sketch.shape[1]
    per = ROWS_DEV // tile
    me = lax.axis_index(AXES).astype(jnp.int32)
    doc_base = lax.axis_index("doc").astype(jnp.int32) * (sketch.shape[0] // tile)

    def swap(v, mask):
        return lax.ppermute(v, AXES, [(i, i ^ mask) for i in range(devices)])

    def swap_y(values):
        return [swap(v, 2 * (k + 1)) for k, v in enumerate(values)]

    n_tiles, count = coords.shape[0], anchors.shape[0]
    is_block = lax.broadcasted_iota(jnp.int32, (2, n_tiles + count), 0) == 0
    anchor = jnp.where(is_block[:, :count], anchors // tile, anchors % tile + doc_base)
    pair = jnp.pad(coords.T, ((0, 0), (0, count))) + jnp.pad(anchor, ((0, 0), (n_tiles, 0)))
    codes = jnp.sum(jnp.where(is_block, encode(n_doc, me, pair, per), (pair - doc_base) << 12), axis=0)
    slots = n_z * n_doc
    away, _, tiles_here, top, low = products(slots, 1, codes, tiles, sketch)
    got = swap(away, n_doc)
    here, token = products(slots, 0, codes, tiles_here, top, low)
    queue = Queue(token)

    def swaps(values):
        return [swap(v, 2 * k if k else 1) for k, v in enumerate(values)]

    def do_spread(groups):
        stay, *sends = spread(queue, groups, n_y, here, got)
        came = []
        for g in range(len(groups)):
            came += swaps(sends[g * n_y : (g + 1) * n_y])
        return [stay, *came]

    def do_join(groups, state, parts, ride_x, cuts):
        keep, rows, *sends = join(queue, groups, n_y, state, parts, ride_x, cuts)
        return keep, rows, [swaps(sends[c * n_y : (c + 1) * n_y]) for c in range(len(cuts))]

    mid = tuple(range(n_z // 2 - 1, 0, -1))
    far_groups = (tuple(range(n_z - 1, n_z // 2 - 1, -1)),)
    near_groups = (mid + (0,),)
    state = do_spread(far_groups)
    pick = functools.partial(pick_kernel, n_tiles)
    part, = queue.call("pick", pick, (shaped((count, width)),), (away, here), (codes,))
    masks = [n_doc << b for b in range((n_term - 1).bit_length())]
    for mask in masks[:-1]:
        part = total(queue, [part, swap(part, mask)])
    n_far, n_mid = len(far_groups[0]), len(mid)
    keep, rows, came = do_join(far_groups, state, (part, swap(part, masks[-1])), True, (n_far,))
    state = do_spread(near_groups)
    rows, *relayed, far = merge(queue, 0, n_far, n_y, keep, came[0], True, (rows,))
    relayed = [swap(v, 2 * n_doc * (dz - n_z // 2)) for v, dz in zip(relayed, far_groups[0])]
    far = swap(total(queue, [far, *relayed]), n_doc * n_z)
    keep, rows, came = do_join(near_groups, state, (rows,), False, (n_mid, 1))
    rows, *sends = merge(queue, 0, n_mid, n_y, keep, came[0], False, (rows,))
    last = [swap(v, 2 * n_doc * dz) for v, dz in zip(sends, mid)]
    gram = gram_of(queue, rows)
    gram = eliminate(queue, gram, 0, TINY)
    near, = merge(queue, n_mid, 1, n_y, keep, came[1], None, (far,))
    gram = eliminate(queue, gram, 1, LONG)
    solve = solver(queue, rows, gram)
    return finish(queue, near, last, rows, solve)


def solution(mesh):
    in_specs = (P(("term", "doc"), None, None), P(("term", "doc"), None), P("doc", None), P())
    out_specs = (P(("term", "doc"), None), P(("term", "doc"), None))
    run = functools.partial(body, mesh.shape["term"], mesh.shape["doc"])
    return jax.shard_map(run, mesh=mesh, in_specs=in_specs, out_specs=out_specs, check_vma=False)
```

```python
import functools

import jax
import jax.numpy as jnp
from jax import lax
from jax.experimental import pallas as pl
from jax.experimental.pallas import tpu as pltpu
from jax.sharding import PartitionSpec as P

ROWS_DEV = 256
UNROLL = 16
FETCHES = 8
AWAY_MIB = 32
HERE_MIB = 24
F32 = jnp.float32
BF16 = jnp.bfloat16
AXES = ("term", "doc")
TOKEN = (8, 128)
LIMIT = pltpu.CompilerParams(vmem_limit_bytes=24 * 2**20)
LARGE = pltpu.CompilerParams(vmem_limit_bytes=32 * 2**20)
TINY = pl.CostEstimate(flops=1, bytes_accessed=1, transcendentals=0)
LONG = pl.CostEstimate(flops=4 * 10**9, bytes_accessed=1, transcendentals=0)
ANY = pl.BlockSpec(memory_space=pl.ANY)
HBM = pl.BlockSpec(memory_space=pltpu.HBM)
SMEM = pl.BlockSpec(memory_space=pltpu.SMEM)
VMEM = pl.BlockSpec(memory_space=pltpu.VMEM)


def shaped(shape, dtype=F32):
    return jax.ShapeDtypeStruct(tuple(shape), dtype)


def split(v):
    hi = v.astype(BF16)
    lo = (v - hi.astype(F32)).astype(BF16)
    return hi, lo


def hdot(a, b, dims):
    return lax.dot_general(a, b, (dims, ((), ())), precision=lax.Precision.HIGHEST, preferred_element_type=F32)


def in_order(kernel, last, _token, *refs):
    kernel(*refs[:last], *refs[last + 1 :])
    refs[last][...] = jnp.zeros_like(refs[last])


class Queue:
    def __init__(self, token):
        self.token = token

    def call(self, name, kernel, out_shape, args, smem=(), cost=TINY):
        got = pl.pallas_call(
            functools.partial(in_order, kernel, len(args) + len(smem)),
            out_shape=(shaped(TOKEN),) + tuple(out_shape),
            in_specs=[VMEM] * (1 + len(args)) + [SMEM] * len(smem),
            out_specs=(VMEM,) * (1 + len(out_shape)),
            compiler_params=LIMIT,
            cost_estimate=cost,
            name=name,
        )(self.token, *args, *smem)
        self.token = got[0]
        return got[1:]


def products_kernel(slots, away, code_ref, *refs):
    if away:
        tiles_in, g_ref, blocks, token, tiles, top_ref, low_ref, order, flag, in_sem = refs
    else:
        tiles, top_ref, low_ref, blocks, token, order, flag = refs
    n_tiles, tile = tiles.shape[:2]
    width = top_ref.shape[1]
    share = n_tiles // FETCHES
    spans = [pl.ds(q * share, share) for q in range(FETCHES)]
    if away:
        loads = [pltpu.make_async_copy(tiles_in.at[span], tiles.at[span], in_sem.at[q]) for q, span in enumerate(spans)]
        for load in loads:
            load.start()
    token[...] = jnp.zeros_like(token)

    def scan(k, count):
        code = code_ref[k]
        order[count] = code | (k << 16)
        return count + (((code >> 10) & 1) == away).astype(jnp.int32)

    counts = [jnp.int32(0)]
    for q in range(FETCHES):
        counts.append(lax.fori_loop(q * share, (q + 1) * share, scan, counts[-1], unroll=8))
    for u in range(UNROLL):
        order[counts[-1] + u] = slots
    blocks[...] = jnp.zeros_like(blocks)
    flag[...] = jnp.zeros_like(flag)
    if away:
        hi, lo = split(g_ref[...])
        top_ref[...] = hi
        low_ref[...] = lo

    def product(code):
        hi, lo = split(tiles[code >> 16])
        rows = pl.ds(pl.multiple_of(((code >> 12) & 15) * tile, tile), tile)
        top = top_ref[rows, :]
        lhs = jnp.concatenate([hi, lo], axis=1)
        both = jnp.dot(lhs, jnp.concatenate([top, top], axis=0), preferred_element_type=F32)
        return both + jnp.dot(hi, low_ref[rows, :], preferred_element_type=F32)

    def several(base, many):
        codes = [order[base + u] for u in range(many)]
        prods = [product(code) for code in codes]
        for code, prod in zip(codes, prods):
            slot = code & 1023
            blocks[slot] += prod
            flag[pl.ds(slot, 1), :] = jnp.full((1, width), ((code >> 11) & 1).astype(F32), F32)

    def group(j, carry):
        several(j * UNROLL, UNROLL)
        return carry

    whole = [count // UNROLL for count in counts[:-1]] + [(counts[-1] + UNROLL - 1) // UNROLL]
    if away:
        for q in range(FETCHES):
            loads[q].wait()
            lax.fori_loop(whole[q], whole[q + 1], group, 0)
    else:
        lax.fori_loop(0, whole[-1], group, 0)
    blocks[slots, pl.ds(0, slots), :] = flag[pl.ds(0, slots), :]


def products(slots, away, codes, tiles, *factors):
    n_tiles, tile = tiles.shape[:2]
    rows, width = factors[0].shape
    outs = [shaped((slots + 1, tile, width)), shaped(TOKEN)]
    scratch = [pltpu.SMEM((n_tiles + UNROLL,), jnp.int32), pltpu.VMEM((slots + 8, width), F32)]
    if away:
        outs += [shaped(tiles.shape)] + [shaped((rows, width), BF16)] * 2
        scratch.append(pltpu.SemaphoreType.DMA((FETCHES,)))
    return pl.pallas_call(
        functools.partial(products_kernel, slots, away),
        out_shape=outs,
        in_specs=[SMEM, HBM if away else VMEM] + [VMEM] * len(factors),
        out_specs=[VMEM] * len(outs),
        scratch_shapes=scratch,
        compiler_params=pltpu.CompilerParams(vmem_limit_bytes=(AWAY_MIB if away else HERE_MIB) * 2**20),
        cost_estimate=pl.CostEstimate(flops=8 * 10**9, bytes_accessed=5 * 2**20, transcendentals=0),
        name="products_away" if away else "products_here",
    )(codes, tiles, *factors)


def encode(n_doc, me, block, per):
    rel = lax.bitwise_xor(block // per, me)
    core = (rel // n_doc) & 1
    slot = (rel // (2 * n_doc)) * n_doc + (rel & (n_doc - 1))
    return slot | (core << 10) | ((block % per) << 11)


def pick_kernel(n_tiles, away, here, code_ref, out):
    slots = away.shape[0] - 1
    for i in range(out.shape[0]):
        code = code_ref[n_tiles + i]
        slot, row = code & 1023, code >> 12
        bit = ((code >> 11) & 1).astype(F32)
        other = ((code >> 10) & 1) == 1
        value = jnp.where(other, away[slot, pl.ds(row, 1), :], here[slot, pl.ds(row, 1), :])
        which = jnp.where(other, away[slots, pl.ds(slot, 1), :], here[slots, pl.ds(slot, 1), :])
        out[i : i + 1, :] = jnp.where(which == bit, value, 0.0)


def spread_kernel(groups, n_y, own, got, stay, *sends):
    slots = own.shape[0] - 1
    half = own.shape[1] // 2
    n_x = sum(len(zs) for zs in groups) * 2 * n_y
    i = 0
    for g, zs in enumerate(groups):
        send_x, *send_y = sends[g * n_y : (g + 1) * n_y]
        for j, dz in enumerate(zs):
            for dy in range(n_y):
                for dx in range(2):
                    slot = (dz * n_y + dy) * 2 + dx
                    a, b = own[slot], got[slot]
                    up_a = a * own[slots, pl.ds(slot, 1), :]
                    up_b = b * got[slots, pl.ds(slot, 1), :]
                    for s, value in enumerate(((a - up_a) + (b - up_b), up_a + up_b)):
                        if dx:
                            send_x[2 * (j * n_y + dy) + s] = value[:half]
                        else:
                            stay[2 * (i * n_y + dy) + s] = value[:half]
                        if dy:
                            send_y[dy - 1][2 * (j * 2 + dx) + s] = value[half:]
                        else:
                            stay[n_x + 2 * (i * 2 + dx) + s] = value[half:]
            i += 1


def spread(queue, groups, n_y, own, got):
    half, width = own.shape[1] // 2, own.shape[2]
    n = sum(len(zs) for zs in groups)
    outs = [shaped((n * (2 * n_y + 4), half, width))]
    for zs in groups:
        outs += [shaped((len(zs) * 2 * n_y, half, width))] + [shaped((len(zs) * 4, half, width))] * (n_y - 1)
    return queue.call("spread", functools.partial(spread_kernel, groups, n_y), outs, (own, got))


def join_kernel(groups, n_y, n_parts, ride_x, cuts, stay, *refs):
    n = sum(len(zs) for zs in groups)
    came = refs[: len(groups) * n_y]
    parts = refs[len(came) : len(came) + n_parts]
    keep, *sends = refs[len(came) + n_parts :]
    if n_parts:
        rows, *sends = sends
    at = [(c, m) for c, cut in enumerate(cuts) for m in range(cut)]
    n_x = n * 2 * n_y
    i = 0
    for g, zs in enumerate(groups):
        got_x, *got_y = came[g * n_y : (g + 1) * n_y]
        for j in range(len(zs)):
            cut, m = at[i]
            send_x, *send_y = sends[cut * n_y : (cut + 1) * n_y]
            for s in range(2):
                for dy in range(n_y):
                    value = stay[2 * (i * n_y + dy) + s] + got_x[2 * (j * n_y + dy) + s]
                    if dy:
                        send_y[dy - 1][2 * m + s] = value
                    else:
                        keep[4 * i + s] = value
                for dx in range(2):
                    value = stay[n_x + 2 * (i * 2 + dx) + s]
                    for ref in got_y:
                        value = value + ref[2 * (j * 2 + dx) + s]
                    if dx:
                        send_x[2 * m + s] = value
                    else:
                        keep[4 * i + 2 + s] = value
            i += 1
    if n_parts:
        total = parts[0][...]
        for ref in parts[1:]:
            total = total + ref[...]
        rows[...] = total
        for ref in sends[:1] if ride_x else sends[1:n_y]:
            ref[2 * cuts[0]] = total


def join(queue, groups, n_y, state, parts, ride_x, cuts):
    stay = state[0]
    half, width = stay.shape[1:]
    n = sum(len(zs) for zs in groups)
    outs = [shaped((4 * n, half, width))] + [shaped((half, width))] * bool(parts)
    for c, cut in enumerate(cuts):
        outs += [shaped((2 * cut + (1 if c == 0 and parts and ride_x == (k == 0) else 0), half, width)) for k in range(n_y)]
    kernel = functools.partial(join_kernel, groups, n_y, len(parts), ride_x, cuts)
    return queue.call("join", kernel, outs, (*state, *parts))


def merge_kernel(start, n, n_y, ride, keep, got_x, *refs):
    got_y, refs = refs[: n_y - 1], refs[n_y - 1 :]
    if ride is None:
        far, outs = refs[:-n], refs[-n:]
    else:
        far, (rows, total, *outs) = (), refs
        value = rows[...]
        for ref in [got_x] if ride else got_y:
            value = value + ref[2 * n]
        total[...] = value
    for i, out in enumerate(outs):
        for s in range(2):
            x = keep[4 * (start + i) + s]
            y = keep[4 * (start + i) + 2 + s] + got_x[2 * i + s]
            for ref in got_y:
                x = x + ref[2 * i + s]
            for ref in far:
                x = x + ref[s]
                y = y + ref[2 + s]
            out[s] = x
            out[2 + s] = y


def merge(queue, start, n, n_y, keep, came, ride, more):
    outs = (shaped((4,) + keep.shape[1:]),) * n
    if ride is not None:
        outs = (shaped(more[0].shape),) + outs
    return queue.call("merge", functools.partial(merge_kernel, start, n, n_y, ride), outs, (keep, *came, *more))


def total_kernel(*refs):
    total = refs[0][...]
    for ref in refs[1:-1]:
        total = total + ref[...]
    refs[-1][...] = total


def total(queue, values):
    return queue.call("total", total_kernel, (shaped(values[0].shape),), values)[0]


def gram_kernel(rows_ref, gram_ref):
    rows = rows_ref[...]
    count = rows.shape[0]
    gram = hdot(rows, rows, ((1,), (1,)))
    diagonal = lax.broadcasted_iota(jnp.int32, (count, count), 0) == lax.broadcasted_iota(jnp.int32, (count, count), 1)
    ridge = 0.001 * jnp.sum(jnp.where(diagonal, gram, 0.0)) / count
    gram_ref[...] = jnp.where(diagonal, gram + ridge, gram)


def gram_of(queue, rows):
    return queue.call("gram", gram_kernel, (shaped((rows.shape[0],) * 2),), (rows,))[0]


def eliminate_kernel(lo, hi, given, out):
    m = given[...]
    count = m.shape[0]
    at_row = lax.broadcasted_iota(jnp.int32, (count, count), 0)
    at_col = lax.broadcasted_iota(jnp.int32, (count, count), 1)
    for k in range(lo, hi):
        row = m[k : k + 1, :]
        col = m[:, k : k + 1]
        scale = 1.0 / m[k : k + 1, k : k + 1]
        row = jnp.where(at_col[:1] == k, 1.0, row) * scale
        m = jnp.where(at_row == k, row, jnp.where(at_col == k, 0.0, m) - col * row)
    out[...] = m


def eliminate(queue, m, part, cost):
    half = m.shape[0] // 2
    kernel = functools.partial(eliminate_kernel, part * half, (part + 1) * half)
    return queue.call("eliminate", kernel, (shaped(m.shape),), (m,), cost=cost)[0]


def solver_kernel(rows, inv, out):
    out[...] = hdot(rows[...], inv[...], ((0,), (0,)))


def solver(queue, rows, inv):
    return queue.call("solver", solver_kernel, (shaped(rows.shape[::-1]),), (rows, inv))[0]


def finish_kernel(n_far, near, *refs):
    x, y = near[:2], near[2:]
    for ref in refs[:n_far]:
        x = x + ref[:2]
        y = y + ref[2:]
    rows_ref, solve_ref, coef_ref, res_ref = refs[n_far:]
    owned = jnp.concatenate([x[0], y[0], x[1], y[1]], axis=0)
    coef = hdot(owned, solve_ref[...], ((1,), (0,)))
    res_ref[...] = owned - hdot(coef, rows_ref[...], ((1,), (0,)))
    coef_ref[...] = coef.T


def finish(queue, near, far, rows, solve):
    half, width = near.shape[1:]
    outs = (shaped((rows.shape[0], 4 * half)), shaped((4 * half, width)))
    coef, res = queue.call("finish", functools.partial(finish_kernel, len(far)), outs, (near, *far, rows, solve))
    return coef.T, res


def body(n_term, n_doc, tiles, coords, sketch, anchors):
    devices = n_term * n_doc
    n_y, n_z = n_doc // 2, n_term // 2
    tile, width = tiles.shape[1], sketch.shape[1]
    per = ROWS_DEV // tile
    me = lax.axis_index(AXES).astype(jnp.int32)
    doc_base = lax.axis_index("doc").astype(jnp.int32) * (sketch.shape[0] // tile)

    def swap(v, mask):
        return lax.ppermute(v, AXES, [(i, i ^ mask) for i in range(devices)])

    def swap_y(values):
        return [swap(v, 2 * (k + 1)) for k, v in enumerate(values)]

    n_tiles, count = coords.shape[0], anchors.shape[0]
    is_block = lax.broadcasted_iota(jnp.int32, (2, n_tiles + count), 0) == 0
    anchor = jnp.where(is_block[:, :count], anchors // tile, anchors % tile + doc_base)
    pair = jnp.pad(coords.T, ((0, 0), (0, count))) + jnp.pad(anchor, ((0, 0), (n_tiles, 0)))
    codes = jnp.sum(jnp.where(is_block, encode(n_doc, me, pair, per), (pair - doc_base) << 12), axis=0)
    slots = n_z * n_doc
    away, _, tiles_here, top, low = products(slots, 1, codes, tiles, sketch)
    got = swap(away, n_doc)
    here, token = products(slots, 0, codes, tiles_here, top, low)
    queue = Queue(token)

    def swaps(values):
        return [swap(v, 2 * k if k else 1) for k, v in enumerate(values)]

    def do_spread(groups):
        stay, *sends = spread(queue, groups, n_y, here, got)
        came = []
        for g in range(len(groups)):
            came += swaps(sends[g * n_y : (g + 1) * n_y])
        return [stay, *came]

    def do_join(groups, state, parts, ride_x, cuts):
        keep, *sends = join(queue, groups, n_y, state, parts, ride_x, cuts)
        rows = sends.pop(0) if parts else None
        return keep, rows, [swaps(sends[c * n_y : (c + 1) * n_y]) for c in range(len(cuts))]

    mid = tuple(range(n_z // 2 - 1, 0, -1))
    far_groups = (tuple(range(n_z - 1, n_z // 2 - 1, -1)),)
    state = do_spread(far_groups)
    pick = functools.partial(pick_kernel, n_tiles)
    part, = queue.call("pick", pick, (shaped((count, width)),), (away, here), (codes,))
    masks = [n_doc << b for b in range((n_term - 1).bit_length())]
    for mask in masks[:-1]:
        part = total(queue, [part, swap(part, mask)])
    n_far, n_mid = len(far_groups[0]), len(mid)
    keep, rows, came = do_join(far_groups, state, (part, swap(part, masks[-1])), True, (n_far,))
    mid_state = do_spread((mid,))
    near_state = do_spread(((0,),))
    rows, *relayed, far = merge(queue, 0, n_far, n_y, keep, came[0], True, (rows,))
    relayed = [swap(v, 2 * n_doc * (dz - n_z // 2)) for v, dz in zip(relayed, far_groups[0])]
    mid_keep, rows, mid_came = do_join((mid,), mid_state, (rows,), False, (n_mid,))
    far = swap(total(queue, [far, *relayed]), n_doc * n_z)
    keep, _, came = do_join(((0,),), near_state, (), None, (1,))
    rows, *sends = merge(queue, 0, n_mid, n_y, mid_keep, mid_came[0], False, (rows,))
    last = [swap(v, 2 * n_doc * dz) for v, dz in zip(sends, mid)]
    gram = gram_of(queue, rows)
    gram = eliminate(queue, gram, 0, TINY)
    near, = merge(queue, 0, 1, n_y, keep, came[0], None, (far,))
    gram = eliminate(queue, gram, 1, LONG)
    solve = solver(queue, rows, gram)
    return finish(queue, near, last, rows, solve)


def solution(mesh):
    in_specs = (P(("term", "doc"), None, None), P(("term", "doc"), None), P("doc", None), P())
    out_specs = (P(("term", "doc"), None), P(("term", "doc"), None))
    run = functools.partial(body, mesh.shape["term"], mesh.shape["doc"])
    return jax.shard_map(run, mesh=mesh, in_specs=in_specs, out_specs=out_specs, check_vma=False)
```

```python
import functools

import jax
import jax.numpy as jnp
from jax import lax
from jax.experimental import pallas as pl
from jax.experimental.pallas import tpu as pltpu
from jax.sharding import PartitionSpec as P

ROWS_DEV = 256
UNROLL = 16
FETCHES = 8
AWAY_MIB = 32
HERE_MIB = 24
F32 = jnp.float32
BF16 = jnp.bfloat16
AXES = ("term", "doc")
TOKEN = (8, 128)
LIMIT = pltpu.CompilerParams(vmem_limit_bytes=24 * 2**20)
LARGE = pltpu.CompilerParams(vmem_limit_bytes=32 * 2**20)
TINY = pl.CostEstimate(flops=1, bytes_accessed=1, transcendentals=0)
LONG = pl.CostEstimate(flops=4 * 10**9, bytes_accessed=1, transcendentals=0)
ANY = pl.BlockSpec(memory_space=pl.ANY)
HBM = pl.BlockSpec(memory_space=pltpu.HBM)
SMEM = pl.BlockSpec(memory_space=pltpu.SMEM)
VMEM = pl.BlockSpec(memory_space=pltpu.VMEM)


def shaped(shape, dtype=F32):
    return jax.ShapeDtypeStruct(tuple(shape), dtype)


def split(v):
    hi = v.astype(BF16)
    lo = (v - hi.astype(F32)).astype(BF16)
    return hi, lo


def hdot(a, b, dims):
    return lax.dot_general(a, b, (dims, ((), ())), precision=lax.Precision.HIGHEST, preferred_element_type=F32)


def in_order(kernel, last, _token, *refs):
    kernel(*refs[:last], *refs[last + 1 :])
    refs[last][...] = jnp.zeros_like(refs[last])


class Queue:
    def __init__(self, token):
        self.token = token

    def call(self, name, kernel, out_shape, args, smem=(), cost=TINY):
        got = pl.pallas_call(
            functools.partial(in_order, kernel, len(args) + len(smem)),
            out_shape=(shaped(TOKEN),) + tuple(out_shape),
            in_specs=[VMEM] * (1 + len(args)) + [SMEM] * len(smem),
            out_specs=(VMEM,) * (1 + len(out_shape)),
            compiler_params=LIMIT,
            cost_estimate=cost,
            name=name,
        )(self.token, *args, *smem)
        self.token = got[0]
        return got[1:]


def products_kernel(slots, away, code_ref, *refs):
    if away:
        tiles_in, g_ref, blocks, token, tiles, top_ref, low_ref, order, flag, in_sem = refs
    else:
        tiles, top_ref, low_ref, blocks, token, order, flag = refs
    n_tiles, tile = tiles.shape[:2]
    width = top_ref.shape[1]
    share = n_tiles // FETCHES
    spans = [pl.ds(q * share, share) for q in range(FETCHES)]
    if away:
        loads = [pltpu.make_async_copy(tiles_in.at[span], tiles.at[span], in_sem.at[q]) for q, span in enumerate(spans)]
        for load in loads:
            load.start()
    token[...] = jnp.zeros_like(token)

    def scan(k, count):
        code = code_ref[k]
        order[count] = code | (k << 16)
        return count + (((code >> 10) & 1) == away).astype(jnp.int32)

    counts = [jnp.int32(0)]
    for q in range(FETCHES):
        counts.append(lax.fori_loop(q * share, (q + 1) * share, scan, counts[-1], unroll=8))
    for u in range(UNROLL):
        order[counts[-1] + u] = slots
    blocks[...] = jnp.zeros_like(blocks)
    flag[...] = jnp.zeros_like(flag)
    if away:
        hi, lo = split(g_ref[...])
        top_ref[...] = hi
        low_ref[...] = lo

    def product(code):
        hi, lo = split(tiles[code >> 16])
        rows = pl.ds(pl.multiple_of(((code >> 12) & 15) * tile, tile), tile)
        top = top_ref[rows, :]
        lhs = jnp.concatenate([hi, lo], axis=1)
        both = jnp.dot(lhs, jnp.concatenate([top, top], axis=0), preferred_element_type=F32)
        return both + jnp.dot(hi, low_ref[rows, :], preferred_element_type=F32)

    def several(base, many):
        codes = [order[base + u] for u in range(many)]
        prods = [product(code) for code in codes]
        for code, prod in zip(codes, prods):
            slot = code & 1023
            blocks[slot] += prod
            flag[pl.ds(slot, 1), :] = jnp.full((1, width), ((code >> 11) & 1).astype(F32), F32)

    def group(j, carry):
        several(j * UNROLL, UNROLL)
        return carry

    whole = [count // UNROLL for count in counts[:-1]] + [(counts[-1] + UNROLL - 1) // UNROLL]
    if away:
        for q in range(FETCHES):
            loads[q].wait()
            lax.fori_loop(whole[q], whole[q + 1], group, 0)
    else:
        lax.fori_loop(0, whole[-1], group, 0)
    blocks[slots, pl.ds(0, slots), :] = flag[pl.ds(0, slots), :]


def products(slots, away, codes, tiles, *factors):
    n_tiles, tile = tiles.shape[:2]
    rows, width = factors[0].shape
    outs = [shaped((slots + 1, tile, width)), shaped(TOKEN)]
    scratch = [pltpu.SMEM((n_tiles + UNROLL,), jnp.int32), pltpu.VMEM((slots + 8, width), F32)]
    if away:
        outs += [shaped(tiles.shape)] + [shaped((rows, width), BF16)] * 2
        scratch.append(pltpu.SemaphoreType.DMA((FETCHES,)))
    return pl.pallas_call(
        functools.partial(products_kernel, slots, away),
        out_shape=outs,
        in_specs=[SMEM, HBM if away else VMEM] + [VMEM] * len(factors),
        out_specs=[VMEM] * len(outs),
        scratch_shapes=scratch,
        compiler_params=pltpu.CompilerParams(vmem_limit_bytes=(AWAY_MIB if away else HERE_MIB) * 2**20),
        cost_estimate=pl.CostEstimate(flops=8 * 10**9, bytes_accessed=5 * 2**20, transcendentals=0),
        name="products_away" if away else "products_here",
    )(codes, tiles, *factors)


def encode(n_doc, me, block, extra, per):
    rel = lax.bitwise_xor(block // per, me)
    core = (rel // n_doc) & 1
    slot = (rel // (2 * n_doc)) * n_doc + (rel & (n_doc - 1))
    return slot | (core << 10) | ((block % per) << 11) | (extra << 12)


def pick_kernel(away, here, code_ref, out):
    slots = away.shape[0] - 1
    for i in range(out.shape[0]):
        code = code_ref[i]
        slot, row = code & 1023, code >> 12
        bit = ((code >> 11) & 1).astype(F32)
        other = ((code >> 10) & 1) == 1
        value = jnp.where(other, away[slot, pl.ds(row, 1), :], here[slot, pl.ds(row, 1), :])
        which = jnp.where(other, away[slots, pl.ds(slot, 1), :], here[slots, pl.ds(slot, 1), :])
        out[i : i + 1, :] = jnp.where(which == bit, value, 0.0)


def spread_kernel(groups, n_y, own, got, stay, *sends):
    slots = own.shape[0] - 1
    half = own.shape[1] // 2
    n_x = sum(len(zs) for zs in groups) * 2 * n_y
    i = 0
    for g, zs in enumerate(groups):
        send_x, *send_y = sends[g * n_y : (g + 1) * n_y]
        for j, dz in enumerate(zs):
            for dy in range(n_y):
                for dx in range(2):
                    slot = (dz * n_y + dy) * 2 + dx
                    a, b = own[slot], got[slot]
                    up_a = a * own[slots, pl.ds(slot, 1), :]
                    up_b = b * got[slots, pl.ds(slot, 1), :]
                    for s, value in enumerate(((a - up_a) + (b - up_b), up_a + up_b)):
                        if dx:
                            send_x[2 * (j * n_y + dy) + s] = value[:half]
                        else:
                            stay[2 * (i * n_y + dy) + s] = value[:half]
                        if dy:
                            send_y[dy - 1][2 * (j * 2 + dx) + s] = value[half:]
                        else:
                            stay[n_x + 2 * (i * 2 + dx) + s] = value[half:]
            i += 1


def spread(queue, groups, n_y, own, got):
    half, width = own.shape[1] // 2, own.shape[2]
    n = sum(len(zs) for zs in groups)
    outs = [shaped((n * (2 * n_y + 4), half, width))]
    for zs in groups:
        outs += [shaped((len(zs) * 2 * n_y, half, width))] + [shaped((len(zs) * 4, half, width))] * (n_y - 1)
    return queue.call("spread", functools.partial(spread_kernel, groups, n_y), outs, (own, got))


def join_kernel(groups, n_y, n_parts, ride_x, cuts, stay, *refs):
    n = sum(len(zs) for zs in groups)
    came = refs[: len(groups) * n_y]
    parts = refs[len(came) : len(came) + n_parts]
    keep, *sends = refs[len(came) + n_parts :]
    if n_parts:
        rows, *sends = sends
    at = [(c, m) for c, cut in enumerate(cuts) for m in range(cut)]
    n_x = n * 2 * n_y
    i = 0
    for g, zs in enumerate(groups):
        got_x, *got_y = came[g * n_y : (g + 1) * n_y]
        for j in range(len(zs)):
            cut, m = at[i]
            send_x, *send_y = sends[cut * n_y : (cut + 1) * n_y]
            for s in range(2):
                for dy in range(n_y):
                    value = stay[2 * (i * n_y + dy) + s] + got_x[2 * (j * n_y + dy) + s]
                    if dy:
                        send_y[dy - 1][2 * m + s] = value
                    else:
                        keep[4 * i + s] = value
                for dx in range(2):
                    value = stay[n_x + 2 * (i * 2 + dx) + s]
                    for ref in got_y:
                        value = value + ref[2 * (j * 2 + dx) + s]
                    if dx:
                        send_x[2 * m + s] = value
                    else:
                        keep[4 * i + 2 + s] = value
            i += 1
    if n_parts:
        total = parts[0][...]
        for ref in parts[1:]:
            total = total + ref[...]
        rows[...] = total
        for ref in sends[:1] if ride_x else sends[1:n_y]:
            ref[2 * cuts[0]] = total


def join(queue, groups, n_y, state, parts, ride_x, cuts):
    stay = state[0]
    half, width = stay.shape[1:]
    n = sum(len(zs) for zs in groups)
    outs = [shaped((4 * n, half, width))] + [shaped((half, width))] * bool(parts)
    for c, cut in enumerate(cuts):
        outs += [shaped((2 * cut + (1 if c == 0 and parts and ride_x == (k == 0) else 0), half, width)) for k in range(n_y)]
    kernel = functools.partial(join_kernel, groups, n_y, len(parts), ride_x, cuts)
    return queue.call("join", kernel, outs, (*state, *parts))


def merge_kernel(start, n, n_y, ride, keep, got_x, *refs):
    got_y, refs = refs[: n_y - 1], refs[n_y - 1 :]
    if ride is None:
        far, outs = refs[:-n], refs[-n:]
    else:
        far, (rows, total, *outs) = (), refs
        value = rows[...]
        for ref in [got_x] if ride else got_y:
            value = value + ref[2 * n]
        total[...] = value
    for i, out in enumerate(outs):
        for s in range(2):
            x = keep[4 * (start + i) + s]
            y = keep[4 * (start + i) + 2 + s] + got_x[2 * i + s]
            for ref in got_y:
                x = x + ref[2 * i + s]
            for ref in far:
                x = x + ref[s]
                y = y + ref[2 + s]
            out[s] = x
            out[2 + s] = y


def merge(queue, start, n, n_y, keep, came, ride, more):
    outs = (shaped((4,) + keep.shape[1:]),) * n
    if ride is not None:
        outs = (shaped(more[0].shape),) + outs
    return queue.call("merge", functools.partial(merge_kernel, start, n, n_y, ride), outs, (keep, *came, *more))


def total_kernel(*refs):
    total = refs[0][...]
    for ref in refs[1:-1]:
        total = total + ref[...]
    refs[-1][...] = total


def total(queue, values):
    return queue.call("total", total_kernel, (shaped(values[0].shape),), values)[0]


def gram_kernel(rows_ref, gram_ref):
    rows = rows_ref[...]
    count = rows.shape[0]
    gram = hdot(rows, rows, ((1,), (1,)))
    diagonal = lax.broadcasted_iota(jnp.int32, (count, count), 0) == lax.broadcasted_iota(jnp.int32, (count, count), 1)
    ridge = 0.001 * jnp.sum(jnp.where(diagonal, gram, 0.0)) / count
    gram_ref[...] = jnp.where(diagonal, gram + ridge, gram)


def gram_of(queue, rows):
    return queue.call("gram", gram_kernel, (shaped((rows.shape[0],) * 2),), (rows,))[0]


def eliminate_kernel(lo, hi, given, out):
    m = given[...]
    count = m.shape[0]
    at_row = lax.broadcasted_iota(jnp.int32, (count, count), 0)
    at_col = lax.broadcasted_iota(jnp.int32, (count, count), 1)
    for k in range(lo, hi):
        row = m[k : k + 1, :]
        col = m[:, k : k + 1]
        scale = 1.0 / m[k : k + 1, k : k + 1]
        row = jnp.where(at_col[:1] == k, 1.0, row) * scale
        m = jnp.where(at_row == k, row, jnp.where(at_col == k, 0.0, m) - col * row)
    out[...] = m


def eliminate(queue, m, part, cost):
    half = m.shape[0] // 2
    kernel = functools.partial(eliminate_kernel, part * half, (part + 1) * half)
    return queue.call("eliminate", kernel, (shaped(m.shape),), (m,), cost=cost)[0]


def solver_kernel(rows, inv, out):
    out[...] = hdot(rows[...], inv[...], ((0,), (0,)))


def solver(queue, rows, inv):
    return queue.call("solver", solver_kernel, (shaped(rows.shape[::-1]),), (rows, inv))[0]


def finish_kernel(n_far, near, *refs):
    x, y = near[:2], near[2:]
    for ref in refs[:n_far]:
        x = x + ref[:2]
        y = y + ref[2:]
    rows_ref, solve_ref, coef_ref, res_ref = refs[n_far:]
    owned = jnp.concatenate([x[0], y[0], x[1], y[1]], axis=0)
    coef = hdot(owned, solve_ref[...], ((1,), (0,)))
    res_ref[...] = owned - hdot(coef, rows_ref[...], ((1,), (0,)))
    coef_ref[...] = coef.T


def finish(queue, near, far, rows, solve):
    half, width = near.shape[1:]
    outs = (shaped((rows.shape[0], 4 * half)), shaped((4 * half, width)))
    coef, res = queue.call("finish", functools.partial(finish_kernel, len(far)), outs, (near, *far, rows, solve))
    return coef.T, res


def body(n_term, n_doc, tiles, coords, sketch, anchors):
    devices = n_term * n_doc
    n_y, n_z = n_doc // 2, n_term // 2
    tile, width = tiles.shape[1], sketch.shape[1]
    per = ROWS_DEV // tile
    me = lax.axis_index(AXES).astype(jnp.int32)
    doc_base = lax.axis_index("doc").astype(jnp.int32) * (sketch.shape[0] // tile)

    def swap(v, mask):
        return lax.ppermute(v, AXES, [(i, i ^ mask) for i in range(devices)])

    def swap_y(values):
        return [swap(v, 2 * (k + 1)) for k, v in enumerate(values)]

    count = anchors.shape[0]
    codes = encode(n_doc, me, coords[:, 0], coords[:, 1] - doc_base, per)
    anchor_codes = encode(n_doc, me, anchors // tile, anchors % tile, per)
    slots = n_z * n_doc
    away, _, tiles_here, top, low = products(slots, 1, codes, tiles, sketch)
    got = swap(away, n_doc)
    here, token = products(slots, 0, codes, tiles_here, top, low)
    queue = Queue(token)

    def swaps(values):
        return [swap(v, 2 * k if k else 1) for k, v in enumerate(values)]

    def do_spread(groups):
        stay, *sends = spread(queue, groups, n_y, here, got)
        came = []
        for g in range(len(groups)):
            came += swaps(sends[g * n_y : (g + 1) * n_y])
        return [stay, *came]

    def do_join(groups, state, parts, ride_x, cuts):
        keep, *sends = join(queue, groups, n_y, state, parts, ride_x, cuts)
        rows = sends.pop(0) if parts else None
        return keep, rows, [swaps(sends[c * n_y : (c + 1) * n_y]) for c in range(len(cuts))]

    mid = tuple(range(n_z // 2 - 1, 0, -1))
    far_groups = (tuple(range(n_z - 1, n_z // 2 - 1, -1)),)
    state = do_spread(far_groups)
    part, = queue.call("pick", pick_kernel, (shaped((count, width)),), (away, here), (anchor_codes,))
    masks = [n_doc << b for b in range((n_term - 1).bit_length())]
    for mask in masks[:-1]:
        part = total(queue, [part, swap(part, mask)])
    n_far, n_mid = len(far_groups[0]), len(mid)
    keep, rows, came = do_join(far_groups, state, (part, swap(part, masks[-1])), True, (n_far,))
    mid_state = do_spread((mid,))
    near_state = do_spread(((0,),))
    rows, *relayed, far = merge(queue, 0, n_far, n_y, keep, came[0], True, (rows,))
    relayed = [swap(v, 2 * n_doc * (dz - n_z // 2)) for v, dz in zip(relayed, far_groups[0])]
    mid_keep, rows, mid_came = do_join((mid,), mid_state, (rows,), False, (n_mid,))
    far = swap(total(queue, [far, *relayed]), n_doc * n_z)
    keep, _, came = do_join(((0,),), near_state, (), None, (1,))
    rows, *sends = merge(queue, 0, n_mid, n_y, mid_keep, mid_came[0], False, (rows,))
    last = [swap(v, 2 * n_doc * dz) for v, dz in zip(sends, mid)]
    gram = gram_of(queue, rows)
    gram = eliminate(queue, gram, 0, TINY)
    near, = merge(queue, 0, 1, n_y, keep, came[0], None, (far,))
    gram = eliminate(queue, gram, 1, LONG)
    solve = solver(queue, rows, gram)
    return finish(queue, near, last, rows, solve)


def solution(mesh):
    in_specs = (P(("term", "doc"), None, None), P(("term", "doc"), None), P("doc", None), P())
    out_specs = (P(("term", "doc"), None), P(("term", "doc"), None))
    run = functools.partial(body, mesh.shape["term"], mesh.shape["doc"])
    return jax.shard_map(run, mesh=mesh, in_specs=in_specs, out_specs=out_specs, check_vma=False)
```

```python
import functools

import jax
import jax.numpy as jnp
from jax import lax
from jax.experimental import pallas as pl
from jax.experimental.pallas import tpu as pltpu
from jax.sharding import PartitionSpec as P

ROWS_DEV = 256
UNROLL = 16
FETCHES = 8
AWAY_MIB = 32
HERE_MIB = 24
F32 = jnp.float32
BF16 = jnp.bfloat16
AXES = ("term", "doc")
TOKEN = (8, 128)
LIMIT = pltpu.CompilerParams(vmem_limit_bytes=24 * 2**20)
LARGE = pltpu.CompilerParams(vmem_limit_bytes=32 * 2**20)
TINY = pl.CostEstimate(flops=1, bytes_accessed=1, transcendentals=0)
LONG = pl.CostEstimate(flops=4 * 10**9, bytes_accessed=1, transcendentals=0)
ANY = pl.BlockSpec(memory_space=pl.ANY)
HBM = pl.BlockSpec(memory_space=pltpu.HBM)
SMEM = pl.BlockSpec(memory_space=pltpu.SMEM)
VMEM = pl.BlockSpec(memory_space=pltpu.VMEM)


def shaped(shape, dtype=F32):
    return jax.ShapeDtypeStruct(tuple(shape), dtype)


def split(v):
    hi = v.astype(BF16)
    lo = (v - hi.astype(F32)).astype(BF16)
    return hi, lo


def hdot(a, b, dims):
    return lax.dot_general(a, b, (dims, ((), ())), precision=lax.Precision.HIGHEST, preferred_element_type=F32)


def in_order(kernel, last, _token, *refs):
    kernel(*refs[:last], *refs[last + 1 :])
    refs[last][...] = jnp.zeros_like(refs[last])


class Queue:
    def __init__(self, token):
        self.token = token

    def call(self, name, kernel, out_shape, args, smem=(), cost=TINY):
        got = pl.pallas_call(
            functools.partial(in_order, kernel, len(args) + len(smem)),
            out_shape=(shaped(TOKEN),) + tuple(out_shape),
            in_specs=[VMEM] * (1 + len(args)) + [SMEM] * len(smem),
            out_specs=(VMEM,) * (1 + len(out_shape)),
            compiler_params=LIMIT,
            cost_estimate=cost,
            name=name,
        )(self.token, *args, *smem)
        self.token = got[0]
        return got[1:]


def products_kernel(slots, away, code_ref, *refs):
    if away:
        tiles_in, g_ref, blocks, token, tiles, top_ref, low_ref, order, flag, in_sem = refs
    else:
        tiles, top_ref, low_ref, blocks, token, order, flag = refs
    n_tiles, tile = tiles.shape[:2]
    width = top_ref.shape[1]
    share = n_tiles // FETCHES
    spans = [pl.ds(q * share, share) for q in range(FETCHES)]
    if away:
        loads = [pltpu.make_async_copy(tiles_in.at[span], tiles.at[span], in_sem.at[q]) for q, span in enumerate(spans)]
        for load in loads:
            load.start()
    token[...] = jnp.zeros_like(token)

    def scan(k, count):
        code = code_ref[k]
        order[count] = code | (k << 16)
        return count + (((code >> 10) & 1) == away).astype(jnp.int32)

    counts = [jnp.int32(0)]
    for q in range(FETCHES):
        counts.append(lax.fori_loop(q * share, (q + 1) * share, scan, counts[-1], unroll=8))
    for u in range(UNROLL):
        order[counts[-1] + u] = slots
    blocks[...] = jnp.zeros_like(blocks)
    flag[...] = jnp.zeros_like(flag)
    if away:
        hi, lo = split(g_ref[...])
        top_ref[...] = hi
        low_ref[...] = lo

    def product(code):
        hi, lo = split(tiles[code >> 16])
        rows = pl.ds(pl.multiple_of(((code >> 12) & 15) * tile, tile), tile)
        top = top_ref[rows, :]
        lhs = jnp.concatenate([hi, lo], axis=1)
        both = jnp.dot(lhs, jnp.concatenate([top, top], axis=0), preferred_element_type=F32)
        return both + jnp.dot(hi, low_ref[rows, :], preferred_element_type=F32)

    def several(base, many):
        codes = [order[base + u] for u in range(many)]
        prods = [product(code) for code in codes]
        for code, prod in zip(codes, prods):
            slot = code & 1023
            blocks[slot] += prod
            flag[pl.ds(slot, 1), :] = jnp.full((1, width), ((code >> 11) & 1).astype(F32), F32)

    def group(j, carry):
        several(j * UNROLL, UNROLL)
        return carry

    whole = [count // UNROLL for count in counts[:-1]] + [(counts[-1] + UNROLL - 1) // UNROLL]
    if away:
        for q in range(FETCHES):
            loads[q].wait()
            lax.fori_loop(whole[q], whole[q + 1], group, 0)
    else:
        lax.fori_loop(0, whole[-1], group, 0)
    blocks[slots, pl.ds(0, slots), :] = flag[pl.ds(0, slots), :]


def products(slots, away, codes, tiles, *factors):
    n_tiles, tile = tiles.shape[:2]
    rows, width = factors[0].shape
    outs = [shaped((slots + 1, tile, width)), shaped(TOKEN)]
    scratch = [pltpu.SMEM((n_tiles + UNROLL,), jnp.int32), pltpu.VMEM((slots + 8, width), F32)]
    if away:
        outs += [shaped(tiles.shape)] + [shaped((rows, width), BF16)] * 2
        scratch.append(pltpu.SemaphoreType.DMA((FETCHES,)))
    return pl.pallas_call(
        functools.partial(products_kernel, slots, away),
        out_shape=outs,
        in_specs=[SMEM, HBM if away else VMEM] + [VMEM] * len(factors),
        out_specs=[VMEM] * len(outs),
        scratch_shapes=scratch,
        compiler_params=pltpu.CompilerParams(vmem_limit_bytes=(AWAY_MIB if away else HERE_MIB) * 2**20),
        cost_estimate=pl.CostEstimate(flops=8 * 10**9, bytes_accessed=5 * 2**20, transcendentals=0),
        name="products_away" if away else "products_here",
    )(codes, tiles, *factors)


def encode(n_doc, me, block, extra, per):
    rel = lax.bitwise_xor(block // per, me)
    core = (rel // n_doc) & 1
    slot = (rel // (2 * n_doc)) * n_doc + (rel & (n_doc - 1))
    return slot | (core << 10) | ((block % per) << 11) | (extra << 12)


def pick_kernel(away, here, code_ref, out):
    slots = away.shape[0] - 1
    for i in range(out.shape[0]):
        code = code_ref[i]
        slot, row = code & 1023, code >> 12
        bit = ((code >> 11) & 1).astype(F32)
        other = ((code >> 10) & 1) == 1
        value = jnp.where(other, away[slot, pl.ds(row, 1), :], here[slot, pl.ds(row, 1), :])
        which = jnp.where(other, away[slots, pl.ds(slot, 1), :], here[slots, pl.ds(slot, 1), :])
        out[i : i + 1, :] = jnp.where(which == bit, value, 0.0)


def spread_kernel(groups, n_y, own, got, stay, *sends):
    slots = own.shape[0] - 1
    half = own.shape[1] // 2
    n_x = sum(len(zs) for zs in groups) * 2 * n_y
    i = 0
    for g, zs in enumerate(groups):
        send_x, *send_y = sends[g * n_y : (g + 1) * n_y]
        for j, dz in enumerate(zs):
            for dy in range(n_y):
                for dx in range(2):
                    slot = (dz * n_y + dy) * 2 + dx
                    a, b = own[slot], got[slot]
                    up_a = a * own[slots, pl.ds(slot, 1), :]
                    up_b = b * got[slots, pl.ds(slot, 1), :]
                    for s, value in enumerate(((a - up_a) + (b - up_b), up_a + up_b)):
                        if dx:
                            send_x[2 * (j * n_y + dy) + s] = value[:half]
                        else:
                            stay[2 * (i * n_y + dy) + s] = value[:half]
                        if dy:
                            send_y[dy - 1][2 * (j * 2 + dx) + s] = value[half:]
                        else:
                            stay[n_x + 2 * (i * 2 + dx) + s] = value[half:]
            i += 1


def spread(queue, groups, n_y, own, got):
    half, width = own.shape[1] // 2, own.shape[2]
    n = sum(len(zs) for zs in groups)
    outs = [shaped((n * (2 * n_y + 4), half, width))]
    for zs in groups:
        outs += [shaped((len(zs) * 2 * n_y, half, width))] + [shaped((len(zs) * 4, half, width))] * (n_y - 1)
    return queue.call("spread", functools.partial(spread_kernel, groups, n_y), outs, (own, got))


def join_kernel(groups, n_y, n_parts, ride_x, cuts, stay, *refs):
    n = sum(len(zs) for zs in groups)
    came = refs[: len(groups) * n_y]
    parts = refs[len(came) : len(came) + n_parts]
    keep, *sends = refs[len(came) + n_parts :]
    if n_parts:
        rows, *sends = sends
    at = [(c, m) for c, cut in enumerate(cuts) for m in range(cut)]
    n_x = n * 2 * n_y
    i = 0
    for g, zs in enumerate(groups):
        got_x, *got_y = came[g * n_y : (g + 1) * n_y]
        for j in range(len(zs)):
            cut, m = at[i]
            send_x, *send_y = sends[cut * n_y : (cut + 1) * n_y]
            for s in range(2):
                for dy in range(n_y):
                    value = stay[2 * (i * n_y + dy) + s] + got_x[2 * (j * n_y + dy) + s]
                    if dy:
                        send_y[dy - 1][2 * m + s] = value
                    else:
                        keep[4 * i + s] = value
                for dx in range(2):
                    value = stay[n_x + 2 * (i * 2 + dx) + s]
                    for ref in got_y:
                        value = value + ref[2 * (j * 2 + dx) + s]
                    if dx:
                        send_x[2 * m + s] = value
                    else:
                        keep[4 * i + 2 + s] = value
            i += 1
    if n_parts:
        total = parts[0][...]
        for ref in parts[1:]:
            total = total + ref[...]
        rows[...] = total
        for ref in sends[:1] if ride_x else sends[1:n_y]:
            ref[2 * cuts[0]] = total


def join(queue, groups, n_y, state, parts, ride_x, cuts):
    stay = state[0]
    half, width = stay.shape[1:]
    n = sum(len(zs) for zs in groups)
    outs = [shaped((4 * n, half, width))] + [shaped((half, width))] * bool(parts)
    for c, cut in enumerate(cuts):
        outs += [shaped((2 * cut + (1 if c == 0 and parts and ride_x == (k == 0) else 0), half, width)) for k in range(n_y)]
    kernel = functools.partial(join_kernel, groups, n_y, len(parts), ride_x, cuts)
    return queue.call("join", kernel, outs, (*state, *parts))


def merge_kernel(start, n, n_y, ride, keep, got_x, *refs):
    got_y, refs = refs[: n_y - 1], refs[n_y - 1 :]
    if ride is None:
        far, outs = refs[:-n], refs[-n:]
    else:
        far, (rows, total, *outs) = (), refs
        value = rows[...]
        for ref in [got_x] if ride else got_y:
            value = value + ref[2 * n]
        total[...] = value
    for i, out in enumerate(outs):
        for s in range(2):
            x = keep[4 * (start + i) + s]
            y = keep[4 * (start + i) + 2 + s] + got_x[2 * i + s]
            for ref in got_y:
                x = x + ref[2 * i + s]
            for ref in far:
                x = x + ref[s]
                y = y + ref[2 + s]
            out[s] = x
            out[2 + s] = y


def merge(queue, start, n, n_y, keep, came, ride, more):
    outs = (shaped((4,) + keep.shape[1:]),) * n
    if ride is not None:
        outs = (shaped(more[0].shape),) + outs
    return queue.call("merge", functools.partial(merge_kernel, start, n, n_y, ride), outs, (keep, *came, *more))


def total_kernel(*refs):
    total = refs[0][...]
    for ref in refs[1:-1]:
        total = total + ref[...]
    refs[-1][...] = total


def total(queue, values):
    return queue.call("total", total_kernel, (shaped(values[0].shape),), values)[0]


def eliminate_steps(m, lo, hi):
    count = m.shape[0]
    at_row = lax.broadcasted_iota(jnp.int32, (count, count), 0)
    at_col = lax.broadcasted_iota(jnp.int32, (count, count), 1)
    for k in range(lo, hi):
        row = m[k : k + 1, :]
        col = m[:, k : k + 1]
        scale = 1.0 / m[k : k + 1, k : k + 1]
        row = jnp.where(at_col[:1] == k, 1.0, row) * scale
        m = jnp.where(at_row == k, row, jnp.where(at_col == k, 0.0, m) - col * row)
    return m


def gram_kernel(rows_ref, out):
    rows = rows_ref[...]
    count = rows.shape[0]
    gram = hdot(rows, rows, ((1,), (1,)))
    diagonal = lax.broadcasted_iota(jnp.int32, (count, count), 0) == lax.broadcasted_iota(jnp.int32, (count, count), 1)
    ridge = 0.001 * jnp.sum(jnp.where(diagonal, gram, 0.0)) / count
    out[...] = eliminate_steps(jnp.where(diagonal, gram + ridge, gram), 0, count // 2)


def solver_kernel(rows, given, out):
    count = rows.shape[0]
    out[...] = hdot(rows[...], eliminate_steps(given[...], count // 2, count), ((0,), (0,)))


def finish_kernel(n_far, near, *refs):
    x, y = near[:2], near[2:]
    for ref in refs[:n_far]:
        x = x + ref[:2]
        y = y + ref[2:]
    rows_ref, solve_ref, coef_ref, res_ref = refs[n_far:]
    owned = jnp.concatenate([x[0], y[0], x[1], y[1]], axis=0)
    coef = hdot(owned, solve_ref[...], ((1,), (0,)))
    res_ref[...] = owned - hdot(coef, rows_ref[...], ((1,), (0,)))
    coef_ref[...] = coef.T


def finish(queue, near, far, rows, solve):
    half, width = near.shape[1:]
    outs = (shaped((rows.shape[0], 4 * half)), shaped((4 * half, width)))
    coef, res = queue.call("finish", functools.partial(finish_kernel, len(far)), outs, (near, *far, rows, solve))
    return coef.T, res


def body(n_term, n_doc, tiles, coords, sketch, anchors):
    devices = n_term * n_doc
    n_y, n_z = n_doc // 2, n_term // 2
    tile, width = tiles.shape[1], sketch.shape[1]
    per = ROWS_DEV // tile
    me = lax.axis_index(AXES).astype(jnp.int32)
    doc_base = lax.axis_index("doc").astype(jnp.int32) * (sketch.shape[0] // tile)

    def swap(v, mask):
        return lax.ppermute(v, AXES, [(i, i ^ mask) for i in range(devices)])

    def swap_y(values):
        return [swap(v, 2 * (k + 1)) for k, v in enumerate(values)]

    count = anchors.shape[0]
    codes = encode(n_doc, me, coords[:, 0], coords[:, 1] - doc_base, per)
    anchor_codes = encode(n_doc, me, anchors // tile, anchors % tile, per)
    slots = n_z * n_doc
    away, _, tiles_here, top, low = products(slots, 1, codes, tiles, sketch)
    got = swap(away, n_doc)
    here, token = products(slots, 0, codes, tiles_here, top, low)
    queue = Queue(token)

    def swaps(values):
        return [swap(v, 2 * k if k else 1) for k, v in enumerate(values)]

    def do_spread(groups):
        stay, *sends = spread(queue, groups, n_y, here, got)
        came = []
        for g in range(len(groups)):
            came += swaps(sends[g * n_y : (g + 1) * n_y])
        return [stay, *came]

    def do_join(groups, state, parts, ride_x, cuts):
        keep, *sends = join(queue, groups, n_y, state, parts, ride_x, cuts)
        rows = sends.pop(0) if parts else None
        return keep, rows, [swaps(sends[c * n_y : (c + 1) * n_y]) for c in range(len(cuts))]

    mid = tuple(range(n_z // 2 - 1, 0, -1))
    far_groups = (tuple(range(n_z - 1, n_z // 2 - 1, -1)),)
    state = do_spread(far_groups)
    part, = queue.call("pick", pick_kernel, (shaped((count, width)),), (away, here), (anchor_codes,))
    masks = [n_doc << b for b in range((n_term - 1).bit_length())]
    for mask in masks[:-1]:
        part = total(queue, [part, swap(part, mask)])
    n_far, n_mid = len(far_groups[0]), len(mid)
    keep, rows, came = do_join(far_groups, state, (part, swap(part, masks[-1])), True, (n_far,))
    mid_state = do_spread((mid,))
    near_state = do_spread(((0,),))
    rows, *relayed, far = merge(queue, 0, n_far, n_y, keep, came[0], True, (rows,))
    relayed = [swap(v, 2 * n_doc * (dz - n_z // 2)) for v, dz in zip(relayed, far_groups[0])]
    mid_keep, rows, mid_came = do_join((mid,), mid_state, (rows,), False, (n_mid,))
    far = swap(total(queue, [far, *relayed]), n_doc * n_z)
    keep, _, came = do_join(((0,),), near_state, (), None, (1,))
    rows, *sends = merge(queue, 0, n_mid, n_y, mid_keep, mid_came[0], False, (rows,))
    last = [swap(v, 2 * n_doc * dz) for v, dz in zip(sends, mid)]
    half_way, = queue.call("gram", gram_kernel, (shaped((count, count)),), (rows,))
    near, = merge(queue, 0, 1, n_y, keep, came[0], None, (far,))
    solve, = queue.call("solver", solver_kernel, (shaped((width, count)),), (rows, half_way), cost=LONG)
    return finish(queue, near, last, rows, solve)


def solution(mesh):
    in_specs = (P(("term", "doc"), None, None), P(("term", "doc"), None), P("doc", None), P())
    out_specs = (P(("term", "doc"), None), P(("term", "doc"), None))
    run = functools.partial(body, mesh.shape["term"], mesh.shape["doc"])
    return jax.shard_map(run, mesh=mesh, in_specs=in_specs, out_specs=out_specs, check_vma=False)
```
